32 devices in a mesh: trow: 8 (over z, x), tcol: 4 (over y, core).
Axes of the slice: x: 2, y: 2, z: 4, core: 2. Of those that a mesh axis runs over, the one named last changes fastest.
Arguments:
- query: bfloat16 [16, 256, 1152], P('trow', 'tcol'), may hold values from -64 to 64
- key: bfloat16 [16, 256, 1152], P('trow', 'tcol'), may hold values from -6 to 6
- value: bfloat16 [16, 256, 1152], P('trow', 'tcol'), may hold values from -6 to 6
- control: bfloat16 [16, 256, 1152], P('trow', 'tcol'), may hold values from -6 to 6
- kernel: float32 [3, 3, 1152], replicated, may hold values from -3 to 3
- grad_out: bfloat16 [16, 256, 1152], P('trow', 'tcol'), may hold values from -96 to 96
- detail_blocks: int32 [8, 4, 4], P('trow'), may hold values from -1 to 0, as said below
Outputs:
- grad_query: bfloat16 [16, 256, 1152], P('trow', 'tcol')
- grad_key: bfloat16 [16, 256, 1152], P('trow', 'tcol')
- grad_value: bfloat16 [16, 256, 1152], P('trow', 'tcol')
- grad_control: bfloat16 [16, 256, 1152], P('trow', 'tcol')
- grad_kernel: float32 [3, 3, 1152], replicated
The draws below stay inside these ranges and needn't reach their ends.
Inputs may be any that keep to these rules, and one draw needn't show every extreme that they name: `detail_blocks`: entry [i, j, p] is the key block of tile (i, p) that tile (i, j) also attends to, or -1 for none; entry [i, j, j] is -1; each tile names blocks of 1 to 3 other tiles, and in every tile row one tile names a block of each of the other 3 tiles.
All inputs are finite; a program needn't handle non-finite values.
Results may differ from the reference program's by a relative error of at most 0.0095.
Values may be sent and summed in bfloat16 or wider, within the bound.
No kernel may reach another device: no remote copies, remote signals or barrier semaphores. Data moves between devices by JAX's collectives and lax.ppermute only.
A program may use at most 128 MiB of HBM per device.

```python
import jax
import jax.numpy as jnp
from jax import lax

HEADS = 16
HEAD_DIM = 72
D = 1152
TH = 2
TW = 64
BLOCK = 128
BLK_TILE = 1
TILE_ROWS = 8
TILE_COLS = 4
IMG_ROWS = 16
IMG_COLS = 256


def draw_key(key, part):
    shape = (IMG_ROWS, IMG_COLS, D)
    field = jnp.clip(jax.random.normal(jax.random.fold_in(key, 7), shape, jnp.float32), -6.0, 6.0)
    return field.astype(jnp.bfloat16)


def draw_query(key, part):
    shape = (IMG_ROWS, IMG_COLS, D)
    field = jnp.clip(jax.random.normal(jax.random.fold_in(key, 3), shape, jnp.float32), -6.0, 6.0)
    return field.astype(jnp.bfloat16)


def draw_detail_blocks(key, part):
    count_key = jax.random.fold_in(key, 31)
    full_key = jax.random.fold_in(key, 32)
    order_key = jax.random.fold_in(key, 33)
    block_key = jax.random.fold_in(key, 34)
    shape = (TILE_ROWS, TILE_COLS, TILE_COLS)
    counts = jnp.minimum(1 + jax.random.randint(count_key, (TILE_ROWS, TILE_COLS), 0, 4), TILE_COLS - 1)
    full_col = jax.random.randint(full_key, (TILE_ROWS,), 0, TILE_COLS)
    columns = jnp.arange(TILE_COLS, dtype=jnp.int32)
    counts = jnp.where(columns[None, :] == full_col[:, None], TILE_COLS - 1, counts)
    ranking = jax.random.randint(order_key, shape, 0, 1 << 20) * TILE_COLS + columns[None, None, :]
    itself = columns[:, None] == columns[None, :]
    ranking = jnp.where(itself[None, :, :], 1 << 30, ranking)
    places = jnp.argsort(jnp.argsort(ranking, axis=-1), axis=-1)
    picked = places < counts[:, :, None]
    blocks = jax.random.randint(block_key, shape, 0, BLK_TILE)
    return jnp.where(picked, blocks, -1).astype(jnp.int32)


def level_of(own_key, shape, cuts, low, largest):
    def one(axis_at, shards_of):
        steps = jax.random.uniform(jax.random.fold_in(jax.random.fold_in(own_key, 6), axis_at), (shards_of,), jnp.float32, low / len(cuts), largest / len(cuts))
        return jnp.repeat(jnp.exp(steps), shape[axis_at] // shards_of).reshape((-1,) + (1,) * (len(shape) - axis_at - 1))

    loudness = one(*cuts[0])
    for cut in cuts[1:]:
        loudness = loudness * one(*cut)
    return loudness


def centred(rng, dims, spread, bound, shards=(), held_as=jnp.bfloat16):
    level = level_of(rng, dims, shards, -0.22, 0.18) if shards else 1.0
    values = jax.random.normal(rng, dims, jnp.float32) * spread * level
    return jnp.minimum(jnp.maximum(values, -bound), bound).astype(held_as)


def setup_inputs(seed: int = 0) -> dict:
    seeds = jax.random.split(jax.random.key(seed), 8)
    return {
        "query": draw_query(jax.random.fold_in(seeds[7], 71), 0),
        "key": draw_key(jax.random.fold_in(seeds[7], 71), 0),
        "value": centred(seeds[2], (IMG_ROWS, IMG_COLS, D), 1.0, 6.0, ((0, 8), (1, 4))),
        "control": centred(seeds[3], (IMG_ROWS, IMG_COLS, D), 1.0, 6.0, ((0, 8), (1, 4))),
        "kernel": centred(seeds[4], (3, 3, D), 0.5, 3.0, (), jnp.float32),
        "grad_out": centred(seeds[5], (IMG_ROWS, IMG_COLS, D), 16.0, 96.0, ((0, 8), (1, 4))),
        "detail_blocks": draw_detail_blocks(jax.random.fold_in(seeds[7], 71), 0),
    }


NEG = -1e30


def rounded(values):
    narrow = values.astype(jnp.bfloat16)
    narrow = lax.optimization_barrier(narrow)
    return narrow.astype(jnp.float32)


def conv_taps(padded, kernel, rows, cols):
    total = jnp.zeros((rows, cols, padded.shape[2]), jnp.float32)
    for row_off in range(3):
        for col_off in range(3):
            total = total + kernel[row_off, col_off][None, None, :] * padded[row_off:row_off + rows, col_off:col_off + cols]
    return total


def conv_back(padded, kernel, rows, cols):
    total = jnp.zeros((rows, cols, padded.shape[2]), jnp.float32)
    for row_off in range(3):
        for col_off in range(3):
            total = total + kernel[row_off, col_off][None, None, :] * padded[2 - row_off:2 - row_off + rows, 2 - col_off:2 - col_off + cols]
    return total


def to_tiles(image, row_count, col_count):
    rows, cols, channels = image.shape
    tiled = image.reshape(row_count, rows // row_count, col_count, cols // col_count, channels)
    return tiled.transpose(0, 2, 1, 3, 4).reshape(row_count, col_count, (rows // row_count) * (cols // col_count), channels)


def from_tiles(tiles, tile_rows, tile_column_count):
    row_count, col_count, _, channels = tiles.shape
    image = tiles.reshape(row_count, col_count, tile_rows, tile_column_count, channels).transpose(0, 2, 1, 3, 4)
    return image.reshape(row_count * tile_rows, col_count * tile_column_count, channels)


def attend(queries, grads, keys, values, key_live):
    inv_root = HEAD_DIM ** -0.5
    q_three = queries.astype(jnp.float32).reshape(-1, HEADS, HEAD_DIM)
    g_three = grads.astype(jnp.float32).reshape(-1, HEADS, HEAD_DIM)
    k_three = keys.astype(jnp.float32).reshape(-1, HEADS, HEAD_DIM)
    value_three_axes = values.astype(jnp.float32).reshape(-1, HEADS, HEAD_DIM)
    scores = jnp.einsum("qhd,khd->hqk", q_three, k_three) * inv_root
    scores = jnp.where(key_live[None, None, :], scores, NEG)
    row_top = jnp.max(scores, axis=2, keepdims=True)
    raised = jnp.exp(scores - row_top)
    weights = raised / jnp.sum(raised, axis=2, keepdims=True)
    weights_bf = rounded(weights)
    attn_out = jnp.einsum("hqk,khd->qhd", weights_bf, value_three_axes)
    row_delta = jnp.sum(g_three * attn_out, axis=2)
    grad_weights = jnp.einsum("qhd,khd->hqk", g_three, value_three_axes)
    grad_scores = weights * (grad_weights - jnp.transpose(row_delta)[:, :, None])
    grad_scores_bf = rounded(grad_scores)
    grad_q = jnp.einsum("hqk,khd->qhd", grad_scores_bf, k_three) * inv_root
    grad_k = jnp.einsum("hqk,qhd->khd", grad_scores_bf, q_three) * inv_root
    grad_v = jnp.einsum("hqk,qhd->khd", weights_bf, g_three)
    channels = HEADS * HEAD_DIM
    return grad_q.reshape(-1, channels), grad_k.reshape(-1, channels), grad_v.reshape(-1, channels)


def add_tile(accum, piece, tile_row, tile_col, start):
    place = (jnp.asarray(tile_row, jnp.int32), jnp.asarray(tile_col, jnp.int32), jnp.asarray(start, jnp.int32), jnp.zeros((), jnp.int32))
    current = lax.dynamic_slice(accum, place, (1, 1, piece.shape[0], piece.shape[1]))
    return lax.dynamic_update_slice(accum, current + piece[None, None], place)


def reference(query, key, value, control, kernel, grad_out, detail_blocks):
    row_count = TILE_ROWS
    col_count = TILE_COLS
    tile_tokens = TH * TW
    channels = query.shape[2]
    control_pad = jnp.pad(control.astype(jnp.float32), ((1, 1), (1, 1), (0, 0)))
    control_conv = conv_taps(control_pad, kernel, IMG_ROWS, IMG_COLS)
    v_ctrl = (value.astype(jnp.float32) + control_conv).astype(jnp.bfloat16)
    q_tiles = to_tiles(query, row_count, col_count)
    key_tile_stack = to_tiles(key, row_count, col_count)
    v_tiles = to_tiles(v_ctrl, row_count, col_count)
    g_tiles = to_tiles(grad_out, row_count, col_count)
    k_pad = jnp.pad(key_tile_stack, ((1, 1), (0, 0), (0, 0), (0, 0)))
    v_pad = jnp.pad(v_tiles, ((1, 1), (0, 0), (0, 0), (0, 0)))
    zero_acc = jnp.zeros((row_count + 2, col_count, tile_tokens, channels), jnp.float32)

    def visit(carry, index):
        key_acc, value_running_sum = carry
        my_row = index // col_count
        my_col = index % col_count
        key_parts = [k_pad[my_row + 1, my_col], k_pad[my_row, my_col], k_pad[my_row + 2, my_col]]
        value_parts = [v_pad[my_row + 1, my_col], v_pad[my_row, my_col], v_pad[my_row + 2, my_col]]
        live_parts = [jnp.ones((tile_tokens,), bool), jnp.full((tile_tokens,), my_row >= 1), jnp.full((tile_tokens,), my_row + 1 < row_count)]
        starts = []
        peers = []
        for slot in range(col_count - 1):
            peer = (slot + (slot >= my_col)).astype(jnp.int32)
            chosen = detail_blocks[my_row, my_col, peer]
            start = (jnp.maximum(chosen, 0) * BLOCK).astype(jnp.int32)
            key_parts.append(lax.dynamic_slice_in_dim(key_tile_stack[my_row, peer], start, BLOCK, 0))
            value_parts.append(lax.dynamic_slice_in_dim(v_tiles[my_row, peer], start, BLOCK, 0))
            live_parts.append(jnp.full((BLOCK,), chosen >= 0))
            starts.append(start)
            peers.append(peer)
        keys = jnp.concatenate(key_parts, axis=0)
        values = jnp.concatenate(value_parts, axis=0)
        key_live = jnp.concatenate(live_parts, axis=0)
        grad_q, grad_k, grad_v = attend(q_tiles[my_row, my_col], g_tiles[my_row, my_col], keys, values, key_live)
        zero_start = jnp.zeros((), jnp.int32)
        offsets = [(my_row + 1, 0), (my_row, tile_tokens), (my_row + 2, 2 * tile_tokens)]
        for tile_row, first in offsets:
            key_acc = add_tile(key_acc, grad_k[first:first + tile_tokens], tile_row, my_col, zero_start)
            value_running_sum = add_tile(value_running_sum, grad_v[first:first + tile_tokens], tile_row, my_col, zero_start)
        for slot in range(col_count - 1):
            first = 3 * tile_tokens + slot * BLOCK
            key_acc = add_tile(key_acc, rounded(grad_k[first:first + BLOCK]), my_row + 1, peers[slot], starts[slot])
            value_running_sum = add_tile(value_running_sum, rounded(grad_v[first:first + BLOCK]), my_row + 1, peers[slot], starts[slot])
        return (key_acc, value_running_sum), grad_q

    (key_acc, value_running_sum), q_grads = lax.scan(visit, (zero_acc, zero_acc), jnp.arange(row_count * col_count, dtype=jnp.int32))
    grad_query = from_tiles(q_grads.reshape(row_count, col_count, tile_tokens, channels), TH, TW).astype(jnp.bfloat16)
    grad_key = from_tiles(key_acc[1:row_count + 1], TH, TW).astype(jnp.bfloat16)
    grad_value = from_tiles(value_running_sum[1:row_count + 1], TH, TW).astype(jnp.bfloat16)
    grad_value_f = grad_value.astype(jnp.float32)
    value_pad = jnp.pad(grad_value_f, ((1, 1), (1, 1), (0, 0)))
    grad_control = conv_back(value_pad, kernel, IMG_ROWS, IMG_COLS).astype(jnp.bfloat16)
    kernel_rows = []
    for row_off in range(3):
        kernel_cols = []
        for col_off in range(3):
            kernel_cols.append(jnp.sum(control_pad[row_off:row_off + IMG_ROWS, col_off:col_off + IMG_COLS] * grad_value_f, axis=(0, 1)))
        kernel_rows.append(jnp.stack(kernel_cols, axis=0))
    grad_kernel = jnp.stack(kernel_rows, axis=0)
    return grad_query, grad_key, grad_value, grad_control, grad_kernel
```

```python
import functools

import jax
import jax.numpy as jnp
from jax import lax
from jax.experimental import pallas as pl
from jax.experimental.pallas import tpu as pltpu
from jax.sharding import Mesh, PartitionSpec as P

HEADS = 16
HEAD_DIM = 72
ROWS = 2
LANES = 128
HALF = 64
NEG = -1e30
INV_ROOT = HEAD_DIM ** (-0.5)
LOG2E = 1.4426950408889634
BF = jnp.bfloat16
F32 = jnp.float32


def params(mib):
    return pltpu.CompilerParams(vmem_limit_bytes=mib << 20)


def call(body, outs, *args, scratch=(), flops=0, mib=24):
    outs = [jax.ShapeDtypeStruct(shape, dtype) for shape, dtype in outs]
    moved = sum(a.size * a.dtype.itemsize for a in list(args) + outs)
    return pl.pallas_call(
        body,
        out_shape=outs,
        scratch_shapes=list(scratch),
        compiler_params=params(mib),
        cost_estimate=pl.CostEstimate(flops=flops, bytes_accessed=moved, transcendentals=0),
    )(*args)


def pack_body(parts, ch, *refs):
    ins, out = refs[:parts], refs[-1]
    pad = out.shape[2] - ch
    for n, ref in enumerate(ins):
        x = ref[...]
        if ch % 16:
            x = x.astype(F32)
        x = x.T
        for p in range(out.shape[0]):
            piece = x[p * ch : (p + 1) * ch]
            if pad:
                piece = jnp.concatenate([piece, jnp.zeros((pad, LANES), piece.dtype)], axis=0)
            out[p, n] = piece.astype(BF)


def pack_live_body(parts, ch, *refs):
    pack_body(parts, ch, *refs[:parts], refs[-2])
    refs[-1][...] = refs[parts][...]


def unpack_body(parts, ch, x_ref, g_ref, *outs):
    peers = x_ref.shape[0]
    for n in range(parts):
        pieces = [x_ref[p, n] for p in range(peers)]
        if ch % 16:
            pieces = [piece.astype(F32)[:ch] for piece in pieces]
        whole = jnp.concatenate(pieces, axis=0)
        outs[n][...] = whole.T.astype(BF)
    wide = outs[-1].shape[2]
    blocks = g_ref.shape[2]
    acc = outs[-1]
    total = [jnp.zeros((16, LANES), F32) for _ in range(wide // LANES + 2)]
    lane = lax.broadcasted_iota(jnp.int32, (16, LANES), 1)
    for p in range(peers):
        first, off = divmod(p * ch, LANES)
        for b in range(blocks):
            piece = g_ref[p, 0, b].astype(F32) + g_ref[p, 1, b].astype(F32)
            turned = pltpu.roll(piece, off, 1) if off else piece
            total[first + b] = total[first + b] + jnp.where(lane >= off, turned, 0.0)
            if off:
                total[first + b + 1] = total[first + b + 1] + jnp.where(lane < off, turned, 0.0)
    total = jnp.concatenate(total[: wide // LANES], axis=1)
    for a in range(3):
        acc[a] = total[3 * a : 3 * a + 3]


def lane_masks(rows):
    lane = lax.broadcasted_iota(jnp.int32, (rows, LANES), 1)
    col = lane & (HALF - 1)
    return lane >= HALF, col == 0, col == HALF - 1


def col_shifts(tiles, masks):
    _, first, last = masks
    swapped = [pltpu.roll(t, HALF, 1) for t in tiles]
    none = jnp.zeros_like(tiles[0])
    out = []
    for j, t in enumerate(tiles):
        before = swapped[j - 1] if j else none
        after = swapped[j + 1] if j + 1 < len(tiles) else none
        out.append(
            (
                pltpu.roll(jnp.where(last, before, t), 1, 1),
                t,
                pltpu.roll(jnp.where(first, after, t), LANES - 1, 1),
            )
        )
    return out


def conv_rows(rows, coef, masks):
    second = masks[0]
    count = len(rows)
    shifted = [col_shifts(row, masks) for row in rows]
    terms = []
    for i, row in enumerate(shifted):
        use = [i < count - 1, 0 < i < count - 1, i > 0]
        terms.append(
            [
                [
                    sum(coef[3 * a + b] * t[b] for b in range(3)) if use[a] else None
                    for a in range(3)
                ]
                for t in row
            ]
        )
    out = []
    for i in range(1, count - 1):
        line = []
        for j in range(len(rows[0])):
            up = jnp.where(second, terms[i - 1][j][0], terms[i][j][0])
            down = jnp.where(second, terms[i][j][2], terms[i + 1][j][2])
            line.append(terms[i][j][1] + pltpu.roll(up + down, HALF, 1))
        out.append(line)
    return out


def taps(kc_ref, at):
    block = kc_ref[at, :]
    return [jnp.broadcast_to(block[:, t : t + 1], (16, LANES)) for t in range(9)]


def attend_body(
    heads, a_ref, u_ref, d_ref, q_ref, live_ref, ends_ref, kc_ref, dq_ref, up_ref, down_ref, dk_ref, dv_ref,
    kt, vt, acc_k, acc_v,
):
    peers = a_ref.shape[0]
    cols = peers // ROWS
    chp = a_ref.shape[2]
    wide = cols * LANES

    @pl.loop(0, chp // 16)
    def _(step):
        at = pl.ds(pl.multiple_of(step * 16, 16), 16)
        masks = lane_masks(16)
        coef = taps(kc_ref, at)
        rows = (
            [[u_ref[j, 3, at, :].astype(F32) for j in range(cols)]]
            + [[u_ref[j, 2, at, :].astype(F32) for j in range(cols)]]
            + [[a_ref[r * cols + j, 2, at, :].astype(F32) for j in range(cols)] for r in range(ROWS)]
            + [[d_ref[j, 2, at, :].astype(F32) for j in range(cols)]]
            + [[d_ref[j, 3, at, :].astype(F32) for j in range(cols)]]
        )
        conv = conv_rows(rows, coef, masks)
        for j in range(cols):
            span = slice(j * LANES, (j + 1) * LANES)
            for i in range(ROWS + 2):
                if i == 0:
                    k, v = u_ref[j, 0, at, :], u_ref[j, 1, at, :]
                elif i <= ROWS:
                    k, v = a_ref[(i - 1) * cols + j, 0, at, :], a_ref[(i - 1) * cols + j, 1, at, :]
                else:
                    k, v = d_ref[j, 0, at, :], d_ref[j, 1, at, :]
                kt[i, at, span] = k
                vt[i, at, span] = (v.astype(F32) + conv[i][j]).astype(BF)

    acc_k[...] = jnp.zeros_like(acc_k)
    acc_v[...] = jnp.zeros_like(acc_v)
    chan = lax.broadcasted_iota(jnp.int32, (chp, LANES), 0)
    mine = [(chan >= h * HEAD_DIM) & (chan < (h + 1) * HEAD_DIM) for h in range(heads)]

    def spread(x):
        x = x.astype(F32)
        return jnp.concatenate([jnp.where(m, x, 0.0) for m in mine], axis=1).astype(BF)

    def dot(x, y, on_x, on_y):
        return lax.dot_general(
            x, y, (((on_x,), (on_y,)), ((), ())), preferred_element_type=F32
        )

    for r in range(ROWS):

        @pl.loop(0, cols)
        def _(j, r=r):
            tile = r * cols + j
            span = pl.ds(pl.multiple_of(j * LANES, LANES), LANES)
            q = spread(q_ref[tile, 0])
            g = spread(q_ref[tile, 1])
            k = jnp.concatenate([kt[r + 1], kt[r, :, span], kt[r + 2, :, span]], axis=1)
            v = jnp.concatenate([vt[r + 1], vt[r, :, span], vt[r + 2, :, span]], axis=1)
            live = live_ref[tile].astype(F32)
            zero = jnp.zeros((1, LANES), F32)
            bias = jnp.concatenate(
                [live[p : p + 1] for p in range(cols)]
                + [
                    ends_ref[0:1] if r == 0 else zero,
                    ends_ref[1:2] if r == ROWS - 1 else zero,
                ],
                axis=1,
            )
            s = dot(q, k, 0, 0) + bias
            top = jnp.max(s, axis=1, keepdims=True)
            e = jnp.exp2((s - top) * (INV_ROOT * LOG2E))
            w = e * (1.0 / jnp.sum(e, axis=1, keepdims=True))
            gw = dot(g, v, 0, 0)
            delta = jnp.sum(w * gw, axis=1, keepdims=True)
            gs = (w * (gw - delta)).astype(BF)
            dk = dot(q, gs, 1, 0)
            dv = dot(g, w.astype(BF), 1, 0)
            dq = dot(k, gs, 1, 1)
            own = dq[:, :LANES]
            for h in range(1, heads):
                own = jnp.where(mine[h], dq[:, h * LANES : (h + 1) * LANES], own)
            dq_ref[tile] = (own * INV_ROOT).astype(BF)
            for acc, part in ((acc_k, dk), (acc_v, dv)):
                acc[r + 1] += part[:, :wide]
                acc[r, :, span] += part[:, wide : wide + LANES]
                acc[r + 2, :, span] += part[:, wide + LANES :]

    second = lax.broadcasted_iota(jnp.int32, (chp, LANES), 1) >= HALF
    for r in range(ROWS):
        dk_ref[r] = acc_k[r + 1] * INV_ROOT
    dv_ref[...] = acc_v[...]
    for out, i, rim in ((up_ref, 0, 1), (down_ref, ROWS + 1, ROWS)):
        for j in range(cols):
            span = slice(j * LANES, (j + 1) * LANES)
            out[j] = (acc_k[i, :, span] * INV_ROOT).astype(BF)
            out[cols + j] = acc_v[i, :, span].astype(BF)
        for m in range(cols // 2):
            left = acc_v[rim, :, 2 * m * LANES : (2 * m + 1) * LANES]
            right = acc_v[rim, :, (2 * m + 1) * LANES : (2 * m + 2) * LANES]
            if i == 0:
                both = jnp.where(second, pltpu.roll(right, HALF, 1), left)
            else:
                both = jnp.where(second, right, pltpu.roll(left, HALF, 1))
            out[2 * cols + m] = both.astype(BF)


def kernel_grad_body(a_ref, u_ref, d_ref, dv_ref, out_ref):
    cols = a_ref.shape[0] // ROWS
    chp = a_ref.shape[2]

    @pl.loop(0, chp // 16)
    def _(step):
        at = pl.ds(pl.multiple_of(step * 16, 16), 16)
        masks = lane_masks(16)
        second = masks[0]
        rows = (
            [[u_ref[j, 3, at, :].astype(F32) for j in range(cols)]]
            + [[u_ref[j, 2, at, :].astype(F32) for j in range(cols)]]
            + [[a_ref[r * cols + j, 2, at, :].astype(F32) for j in range(cols)] for r in range(ROWS)]
            + [[d_ref[j, 2, at, :].astype(F32) for j in range(cols)]]
            + [[d_ref[j, 3, at, :].astype(F32) for j in range(cols)]]
        )
        shifted = [col_shifts(row, masks) for row in rows]
        acc = [jnp.zeros((16, LANES), F32) for _ in range(9)]
        for i in range(ROWS + 2):
            for j in range(cols):
                g = dv_ref[i, at, j * LANES : (j + 1) * LANES]
                turned = pltpu.roll(g, HALF, 1)
                above, here, below = (shifted[i + n][j] for n in range(3))
                for b in range(3):
                    acc[b] += jnp.where(second, above[b], here[b]) * turned
                    acc[3 + b] += here[b] * g
                    acc[6 + b] += jnp.where(second, here[b], below[b]) * turned
        lane = lax.broadcasted_iota(jnp.int32, (16, LANES), 1)
        out = jnp.zeros((16, LANES), F32)
        for t in range(9):
            out = jnp.where(lane == t, jnp.sum(acc[t], axis=1, keepdims=True), out)
        out_ref[at, :] = out


def finish_body(ch, dq_ref, dk_ref, dv_ref, u_ref, d_ref, kc_ref, gk_ref, out_ref, g_ref):
    cols = dq_ref.shape[0] // ROWS
    chp = dq_ref.shape[1]

    @pl.loop(0, chp // 16)
    def _(step):
        at = pl.ds(pl.multiple_of(step * 16, 16), 16)
        masks = lane_masks(16)
        second = masks[0]
        coef = taps(kc_ref, at)[::-1]

        def from_side(ref, n):
            return ref[n, at, :].astype(F32)

        def rounded(x):
            return x.astype(BF).astype(F32)

        rows = []
        for i in range(ROWS + 2):
            row = []
            for j in range(cols):
                x = dv_ref[i, at, j * LANES : (j + 1) * LANES]
                if i == 0:
                    rim = from_side(u_ref, 2 * cols + j // 2)
                    x = x + (rim if j % 2 else pltpu.roll(rim, HALF, 1))
                elif i == ROWS + 1:
                    rim = from_side(d_ref, 2 * cols + j // 2)
                    x = x + (pltpu.roll(rim, HALF, 1) if j % 2 else rim)
                else:
                    if i == 1:
                        x = x + from_side(u_ref, cols + j)
                    if i == ROWS:
                        x = x + from_side(d_ref, cols + j)
                row.append(rounded(x))
            rows.append(row)
        conv = conv_rows(rows, coef, masks)
        for r in range(ROWS):
            for j in range(cols):
                tile = r * cols + j
                k = dk_ref[r, at, j * LANES : (j + 1) * LANES]
                if r == 0:
                    k = k + from_side(u_ref, j)
                if r == ROWS - 1:
                    k = k + from_side(d_ref, j)
                out_ref[tile, 0, at, :] = dq_ref[tile, at, :]
                out_ref[tile, 1, at, :] = k.astype(BF)
                out_ref[tile, 2, at, :] = rows[r + 1][j].astype(BF)
                out_ref[tile, 3, at, :] = conv[r][j].astype(BF)

    turned = gk_ref[...].T[:16]
    blocks = g_ref.shape[2]
    if blocks * LANES > chp:
        turned = jnp.concatenate([turned, jnp.zeros((16, blocks * LANES - chp), F32)], axis=1)
    lane = lax.broadcasted_iota(jnp.int32, turned.shape, 1)
    turned = jnp.where(lane < ch, turned, 0.0)
    high = turned.astype(BF)
    low = (turned - high.astype(F32)).astype(BF)
    for tile in range(out_ref.shape[0]):
        for b in range(blocks):
            g_ref[tile, 0, b] = high[:, b * LANES : (b + 1) * LANES]
            g_ref[tile, 1, b] = low[:, b * LANES : (b + 1) * LANES]


def per_device(query, key, value, control, kernel, grad_out, detail_blocks):
    shape = query.shape
    channels = shape[2]
    planes = lax.axis_size("z")
    cols = lax.axis_size("c")
    peers = ROWS * cols
    heads = HEADS // peers
    ch = heads * HEAD_DIM
    chp = -(-ch // 16) * 16
    plane = ("x", "c")
    my_z = lax.axis_index("z")
    my_col = lax.axis_index("c")
    me = lax.axis_index("x") * cols + my_col

    def flat(x):
        return x.reshape(LANES, channels)

    def swap(x):
        rows = x.shape[1] * x.shape[2]
        out = lax.all_to_all(x.reshape(peers, rows, LANES), plane, 0, 0, tiled=True)
        return out.reshape(x.shape)

    (sent,) = call(
        functools.partial(pack_body, 3, ch),
        [((peers, 3, chp, LANES), BF)],
        flat(key), flat(value), flat(control),
    )
    mine = swap(sent)
    down_pairs = [(i, i + 1) for i in range(planes - 1)]
    up_pairs = [(i + 1, i) for i in range(planes - 1)]
    first, last = mine[:cols], mine[cols:]
    above = lax.ppermute(jnp.concatenate([last, first[:, 2:]], axis=1), "z", down_pairs)
    below = lax.ppermute(jnp.concatenate([first, last[:, 2:]], axis=1), "z", up_pairs)

    wanted = lax.dynamic_index_in_dim(detail_blocks[0], my_col, 0, keepdims=False)
    named = (wanted >= 0) | (jnp.arange(cols) == my_col)
    bias = jnp.where(named, 0.0, NEG).astype(F32)
    bias = jnp.broadcast_to(jnp.pad(bias, (0, 16 - cols))[:, None], (16, LANES)).astype(BF)
    (sent_q,) = call(
        functools.partial(pack_body, 2, ch),
        [((peers, 2, chp, LANES), BF)],
        flat(query), flat(grad_out),
    )
    got = lax.all_to_all(
        jnp.concatenate(
            [sent_q.reshape(peers, 2 * chp, LANES), jnp.broadcast_to(bias, (peers, 16, LANES))],
            axis=1,
        ),
        plane, 0, 0, tiled=True,
    )
    grads = got[:, : 2 * chp].reshape(peers, 2, chp, LANES)
    live = got[:, 2 * chp :]
    ends = jnp.where(jnp.stack([my_z >= 1, my_z + 1 < planes]), 0.0, NEG).astype(F32)
    ends = jnp.broadcast_to(jnp.pad(ends, (0, 6))[:, None], (8, LANES))
    coefs = lax.dynamic_slice_in_dim(kernel.reshape(9, channels), me * ch, ch, 1)
    coefs = jnp.pad(coefs.T, ((0, chp - ch), (0, LANES - 9)))

    wide = cols * LANES
    side = (2 * cols + cols // 2, chp, LANES)
    flops = 10 * peers * heads * LANES * (wide + 2 * LANES) * 256
    dq, to_up, to_down, dk, dv = call(
        functools.partial(attend_body, heads),
        [
            ((peers, chp, LANES), BF),
            (side, BF),
            (side, BF),
            ((ROWS, chp, wide), F32),
            ((ROWS + 2, chp, wide), F32),
        ],
        mine, above, below, grads, live, ends, coefs,
        scratch=[
            pltpu.VMEM((ROWS + 2, chp, wide), BF),
            pltpu.VMEM((ROWS + 2, chp, wide), BF),
            pltpu.VMEM((ROWS + 2, chp, wide), F32),
            pltpu.VMEM((ROWS + 2, chp, wide), F32),
        ],
        flops=flops,
        mib=32,
    )
    from_below = lax.ppermute(to_up, "z", up_pairs)
    from_above = lax.ppermute(to_down, "z", down_pairs)
    (gk,) = call(kernel_grad_body, [((chp, LANES), F32)], mine, above, below, dv)
    gk = lax.psum(gk, "z")
    blocks = -(-ch // LANES)
    results, gk_sent = call(
        functools.partial(finish_body, ch),
        [((peers, 4, chp, LANES), BF), ((peers, 2, blocks, 16, LANES), BF)],
        dq, dk, dv, from_above, from_below, coefs, gk,
    )
    back = lax.all_to_all(
        jnp.concatenate(
            [results.reshape(peers, 4 * chp, LANES), gk_sent.reshape(peers, 32 * blocks, LANES)],
            axis=1,
        ),
        plane, 0, 0, tiled=True,
    )
    outs = call(
        functools.partial(unpack_body, 4, ch),
        [((LANES, channels), BF)] * 4 + [((3, 3, channels), F32)],
        back[:, : 4 * chp].reshape(peers, 4, chp, LANES),
        back[:, 4 * chp :].reshape(peers, 2, blocks, 16, LANES),
    )
    return tuple(x.reshape(shape) for x in outs[:4]) + (outs[4],)


def solution(mesh):
    trow, tcol = mesh.shape["trow"], mesh.shape["tcol"]
    grid = Mesh(mesh.devices.reshape(trow // ROWS, ROWS, tcol), ("z", "x", "c"))
    tiled = P(("z", "x"), "c", None)
    return jax.shard_map(
        per_device,
        mesh=grid,
        in_specs=(tiled, tiled, tiled, tiled, P(), tiled, P(("z", "x"), None, None)),
        out_specs=(tiled, tiled, tiled, tiled, P()),
        check_vma=False,
    )
```

```python
import functools
import math

import jax
import jax.numpy as jnp
from jax import lax
from jax.experimental import pallas as pl
from jax.experimental.pallas import tpu as pltpu
from jax.sharding import Mesh, PartitionSpec as P

HEADS = 16
HEAD_DIM = 72
ROWS = 2
LANES = 128
HALF = 64
NEG = -1e30
INV_ROOT = HEAD_DIM ** (-0.5)
LOG2E = 1.4426950408889634
BF = jnp.bfloat16
F32 = jnp.float32


def params(mib):
    return pltpu.CompilerParams(vmem_limit_bytes=mib << 20)


def call(body, outs, *args, scratch=(), flops=0, mib=8, keep=(), near=()):
    moved = sum(a.size * a.dtype.itemsize for a in args)
    moved += sum(math.prod(shape) * jnp.dtype(dtype).itemsize for shape, dtype in outs)
    outs = [
        pltpu.VMEM(shape, dtype) if n in keep else jax.ShapeDtypeStruct(shape, dtype)
        for n, (shape, dtype) in enumerate(outs)
    ]
    args = [
        pltpu.with_memory_space_constraint(a, pltpu.VMEM) if n in near else a
        for n, a in enumerate(args)
    ]
    return pl.pallas_call(
        body,
        out_shape=outs,
        scratch_shapes=list(scratch),
        compiler_params=params(mib),
        cost_estimate=pl.CostEstimate(flops=flops, bytes_accessed=moved, transcendentals=0),
    )(*args)


def pack_into(refs, ch, chp, put):
    for n, ref in enumerate(refs):
        x = ref[...]
        if ch % 16:
            x = x.astype(F32)
        x = x.T
        for p in range(x.shape[0] // ch):
            piece = x[p * ch : (p + 1) * ch]
            if chp > ch:
                piece = jnp.concatenate([piece, jnp.zeros((chp - ch, LANES), piece.dtype)], axis=0)
            put(p, n, piece.astype(BF))


def pack_body(ch, *refs):
    out = refs[-1]

    def put(p, n, piece):
        out[p, n] = piece

    pack_into(refs[:-1], ch, out.shape[2], put)


def pack_live_body(ch, chp, query_ref, grad_ref, live_ref, out):
    def put(p, n, piece):
        out[p, n * chp : (n + 1) * chp] = piece

    pack_into((query_ref, grad_ref), ch, chp, put)
    live = live_ref[...].astype(BF)
    for p in range(out.shape[0]):
        out[p, 2 * chp :] = live


def unpack_body(ch, x_ref, *outs):
    peers = x_ref.shape[0]
    for n, out in enumerate(outs):
        pieces = [x_ref[p, n] for p in range(peers)]
        if ch % 16:
            pieces = [piece.astype(F32)[:ch] for piece in pieces]
        out[...] = jnp.concatenate(pieces, axis=0).T.astype(BF)


def unpack_query_body(ch, chp, x_ref, out, gk_ref):
    peers = x_ref.shape[0]
    pieces = [x_ref[p, :chp] for p in range(peers)]
    if ch % 16:
        pieces = [piece.astype(F32)[:ch] for piece in pieces]
    out[...] = jnp.concatenate(pieces, axis=0).T.astype(BF)
    blocks = (x_ref.shape[1] - chp) // 32
    wide = gk_ref.shape[1]
    total = [jnp.zeros((16, LANES), F32) for _ in range(wide // LANES + 2)]
    lane = lax.broadcasted_iota(jnp.int32, (16, LANES), 1)
    for p in range(peers):
        first, off = divmod(p * ch, LANES)
        for b in range(blocks):
            at = chp + 32 * b
            piece = x_ref[p, at : at + 16].astype(F32) + x_ref[p, at + 16 : at + 32].astype(F32)
            turned = pltpu.roll(piece, off, 1) if off else piece
            total[first + b] = total[first + b] + jnp.where(lane >= off, turned, 0.0)
            if off:
                total[first + b + 1] = total[first + b + 1] + jnp.where(lane < off, turned, 0.0)
    gk_ref[...] = jnp.concatenate(total[: wide // LANES], axis=1)


def taps_out_body(x_ref, y_ref, out):
    total = x_ref[...] + y_ref[...]
    for a in range(3):
        out[a] = total[3 * a : 3 * a + 3]


def add_body(x_ref, y_ref, out):
    out[...] = x_ref[...] + y_ref[...]


def lane_masks(rows):
    lane = lax.broadcasted_iota(jnp.int32, (rows, LANES), 1)
    col = lane & (HALF - 1)
    return lane >= HALF, col == 0, col == HALF - 1


def col_shifts(tiles, masks):
    _, first, last = masks
    swapped = [pltpu.roll(t, HALF, 1) for t in tiles]
    none = jnp.zeros_like(tiles[0])
    out = []
    for j, t in enumerate(tiles):
        before = swapped[j - 1] if j else none
        after = swapped[j + 1] if j + 1 < len(tiles) else none
        out.append(
            (
                pltpu.roll(jnp.where(last, before, t), 1, 1),
                t,
                pltpu.roll(jnp.where(first, after, t), LANES - 1, 1),
            )
        )
    return out


def conv_rows(rows, coef, masks):
    second = masks[0]
    count = len(rows)
    shifted = [col_shifts(row, masks) for row in rows]
    terms = []
    for i, row in enumerate(shifted):
        use = [i < count - 1, 0 < i < count - 1, i > 0]
        terms.append(
            [
                [
                    sum(coef[3 * a + b] * t[b] for b in range(3)) if use[a] else None
                    for a in range(3)
                ]
                for t in row
            ]
        )
    out = []
    for i in range(1, count - 1):
        line = []
        for j in range(len(rows[0])):
            up = jnp.where(second, terms[i - 1][j][0], terms[i][j][0])
            down = jnp.where(second, terms[i][j][2], terms[i + 1][j][2])
            line.append(terms[i][j][1] + pltpu.roll(up + down, HALF, 1))
        out.append(line)
    return out


def taps(kc_ref, at):
    block = kc_ref[at, :]
    return [jnp.broadcast_to(block[:, t : t + 1], (16, LANES)) for t in range(9)]


def join_halves(left, right, want_second, second):
    if want_second:
        return jnp.where(second, right, pltpu.roll(left, HALF, 1))
    return jnp.where(second, pltpu.roll(right, HALF, 1), left)


def split_halves(both, odd, have_second):
    return both if odd == have_second else pltpu.roll(both, HALF, 1)


def rim_body(a_ref, up_ref, down_ref):
    cols = a_ref.shape[0] // ROWS
    chp = a_ref.shape[2]
    second = lax.broadcasted_iota(jnp.int32, (chp, LANES), 1) >= HALF
    for out, row, further, want_second in (
        (up_ref, 0, 1, False),
        (down_ref, ROWS - 1, ROWS - 2, True),
    ):
        for j in range(cols):
            for n in range(3):
                out[n * cols + j] = a_ref[row * cols + j, n]
        for m in range(cols // 2):
            left, right = (
                a_ref[further * cols + 2 * m + odd, 2].astype(F32) for odd in range(2)
            )
            out[3 * cols + m] = join_halves(left, right, want_second, second).astype(BF)


def control_rows(a_ref, u_ref, d_ref, at):
    cols = a_ref.shape[0] // ROWS

    def outer(ref, have_second):
        return [
            split_halves(ref[3 * cols + j // 2, at, :].astype(F32), j % 2 == 1, have_second)
            for j in range(cols)
        ]

    def halo(ref):
        return [ref[2 * cols + j, at, :].astype(F32) for j in range(cols)]

    own = [[a_ref[r * cols + j, 2, at, :].astype(F32) for j in range(cols)] for r in range(ROWS)]
    return [outer(u_ref, True), halo(u_ref)] + own + [halo(d_ref), outer(d_ref, False)]


def values_body(a_ref, u_ref, d_ref, kc_ref, vt):
    cols = a_ref.shape[0] // ROWS
    chp = a_ref.shape[2]

    @pl.loop(0, chp // 16)
    def _(step):
        at = pl.ds(pl.multiple_of(step * 16, 16), 16)
        masks = lane_masks(16)
        coef = taps(kc_ref, at)
        rows = control_rows(a_ref, u_ref, d_ref, at)
        conv = conv_rows(rows, coef, masks)
        for j in range(cols):
            span = slice(j * LANES, (j + 1) * LANES)
            for i in range(ROWS + 2):
                if i == 0:
                    v = u_ref[cols + j, at, :]
                elif i <= ROWS:
                    v = a_ref[(i - 1) * cols + j, 1, at, :]
                else:
                    v = d_ref[cols + j, at, :]
                vt[i, at, span] = (v.astype(F32) + conv[i][j]).astype(BF)


def attend_body(heads, q_ref, a_ref, u_ref, d_ref, vt, dq_ref, up_ref, down_ref, dk_ref, acc_v, acc_k):
    peers = q_ref.shape[0]
    cols = peers // ROWS
    chp = vt.shape[1]
    wide = cols * LANES
    acc_k[...] = jnp.zeros_like(acc_k)
    acc_v[...] = jnp.zeros_like(acc_v)
    chan = lax.broadcasted_iota(jnp.int32, (chp, LANES), 0)
    mine = [(chan >= h * HEAD_DIM) & (chan < (h + 1) * HEAD_DIM) for h in range(heads)]

    def spread(x):
        x = x.astype(F32)
        return jnp.concatenate([jnp.where(m, x, 0.0) for m in mine], axis=1).astype(BF)

    def dot(x, y, on_x, on_y):
        return lax.dot_general(
            x, y, (((on_x,), (on_y,)), ((), ())), preferred_element_type=F32
        )

    for r in range(ROWS):

        @pl.loop(0, cols)
        def _(j, r=r):
            tile = r * cols + j
            span = pl.ds(pl.multiple_of(j * LANES, LANES), LANES)
            q = spread(q_ref[tile, :chp])
            g = spread(q_ref[tile, chp : 2 * chp])
            k = jnp.concatenate(
                [a_ref[r * cols + p, 0] for p in range(cols)]
                + [
                    u_ref[j] if r == 0 else a_ref[tile - cols, 0],
                    d_ref[j] if r == ROWS - 1 else a_ref[tile + cols, 0],
                ],
                axis=1,
            )
            v = jnp.concatenate([vt[r + 1], vt[r, :, span], vt[r + 2, :, span]], axis=1)
            live = q_ref[tile, 2 * chp :].astype(F32)
            zero = jnp.zeros((1, LANES), F32)
            bias = jnp.concatenate(
                [live[p : p + 1] for p in range(cols)]
                + [
                    live[cols : cols + 1] if r == 0 else zero,
                    live[cols + 1 : cols + 2] if r == ROWS - 1 else zero,
                ],
                axis=1,
            )
            s = dot(q, k, 0, 0) + bias
            top = jnp.max(s, axis=1, keepdims=True)
            e = jnp.exp2((s - top) * (INV_ROOT * LOG2E))
            w = e * (1.0 / jnp.sum(e, axis=1, keepdims=True))
            gw = dot(g, v, 0, 0)
            delta = jnp.sum(w * gw, axis=1, keepdims=True)
            gs = (w * (gw - delta)).astype(BF)
            dk = dot(q, gs, 1, 0)
            dv = dot(g, w.astype(BF), 1, 0)
            dq = dot(k, gs, 1, 1)
            own = dq[:, :LANES]
            for h in range(1, heads):
                own = jnp.where(mine[h], dq[:, h * LANES : (h + 1) * LANES], own)
            dq_ref[tile] = (own * INV_ROOT).astype(BF)
            for acc, part in ((acc_k, dk), (acc_v, dv)):
                acc[r + 1] += part[:, :wide]
                acc[r, :, span] += part[:, wide : wide + LANES]
                acc[r + 2, :, span] += part[:, wide + LANES :]

    second = lax.broadcasted_iota(jnp.int32, (chp, LANES), 1) >= HALF
    for r in range(ROWS):
        dk_ref[r] = acc_k[r + 1] * INV_ROOT
    for out, i, rim in ((up_ref, 0, 1), (down_ref, ROWS + 1, ROWS)):
        for j in range(cols):
            span = slice(j * LANES, (j + 1) * LANES)
            out[j] = (acc_k[i, :, span] * INV_ROOT).astype(BF)
            out[cols + j] = acc_v[i, :, span].astype(BF)
        for m in range(cols // 2):
            left = acc_v[rim, :, 2 * m * LANES : (2 * m + 1) * LANES]
            right = acc_v[rim, :, (2 * m + 1) * LANES : (2 * m + 2) * LANES]
            both = join_halves(left, right, i != 0, second)
            out[2 * cols + m] = both.astype(BF)


def kernel_grad_body(ch, dq_ref, a_ref, u_ref, d_ref, dv_ref, out_ref, sums):
    cols = a_ref.shape[0] // ROWS
    chp = a_ref.shape[2]

    @pl.loop(0, chp // 16)
    def _(step):
        at = pl.ds(pl.multiple_of(step * 16, 16), 16)
        masks = lane_masks(16)
        second = masks[0]
        rows = control_rows(a_ref, u_ref, d_ref, at)
        shifted = [col_shifts(row, masks) for row in rows]
        acc = [jnp.zeros((16, LANES), F32) for _ in range(9)]
        for i in range(ROWS + 2):
            for j in range(cols):
                g = dv_ref[i, at, j * LANES : (j + 1) * LANES]
                turned = pltpu.roll(g, HALF, 1)
                above, here, below = (shifted[i + n][j] for n in range(3))
                for b in range(3):
                    acc[b] += jnp.where(second, above[b], here[b]) * turned
                    acc[3 + b] += here[b] * g
                    acc[6 + b] += jnp.where(second, here[b], below[b]) * turned
        lane = lax.broadcasted_iota(jnp.int32, (16, LANES), 1)
        out = jnp.zeros((16, LANES), F32)
        for t in range(9):
            out = jnp.where(lane == t, jnp.sum(acc[t], axis=1, keepdims=True), out)
        sums[at, :] = out

    turned = sums[...].T[:16]
    blocks = (out_ref.shape[1] - chp) // 32
    if blocks * LANES > chp:
        turned = jnp.concatenate([turned, jnp.zeros((16, blocks * LANES - chp), F32)], axis=1)
    lane = lax.broadcasted_iota(jnp.int32, turned.shape, 1)
    turned = jnp.where(lane < ch, turned, 0.0)
    high = turned.astype(BF)
    low = (turned - high.astype(F32)).astype(BF)
    for tile in range(out_ref.shape[0]):
        out_ref[tile, :chp] = dq_ref[tile]
        for b in range(blocks):
            at = chp + 32 * b
            out_ref[tile, at : at + 16] = high[:, b * LANES : (b + 1) * LANES]
            out_ref[tile, at + 16 : at + 32] = low[:, b * LANES : (b + 1) * LANES]


def finish_body(dk_ref, dv_ref, u_ref, d_ref, kc_ref, out_ref):
    cols = out_ref.shape[0] // ROWS
    chp = out_ref.shape[2]

    @pl.loop(0, chp // 16)
    def _(step):
        at = pl.ds(pl.multiple_of(step * 16, 16), 16)
        masks = lane_masks(16)
        second = masks[0]
        coef = taps(kc_ref, at)[::-1]

        def from_side(ref, n):
            return ref[n, at, :].astype(F32)

        def rounded(x):
            return x.astype(BF).astype(F32)

        rows = []
        for i in range(ROWS + 2):
            row = []
            for j in range(cols):
                x = dv_ref[i, at, j * LANES : (j + 1) * LANES]
                if i == 0:
                    rim = from_side(u_ref, 2 * cols + j // 2)
                    x = x + split_halves(rim, j % 2 == 1, True)
                elif i == ROWS + 1:
                    rim = from_side(d_ref, 2 * cols + j // 2)
                    x = x + split_halves(rim, j % 2 == 1, False)
                else:
                    if i == 1:
                        x = x + from_side(u_ref, cols + j)
                    if i == ROWS:
                        x = x + from_side(d_ref, cols + j)
                row.append(rounded(x))
            rows.append(row)
        conv = conv_rows(rows, coef, masks)
        for r in range(ROWS):
            for j in range(cols):
                tile = r * cols + j
                k = dk_ref[r, at, j * LANES : (j + 1) * LANES]
                if r == 0:
                    k = k + from_side(u_ref, j)
                if r == ROWS - 1:
                    k = k + from_side(d_ref, j)
                out_ref[tile, 0, at, :] = k.astype(BF)
                out_ref[tile, 1, at, :] = rows[r + 1][j].astype(BF)
                out_ref[tile, 2, at, :] = conv[r][j].astype(BF)


def per_device(query, key, value, control, kernel, grad_out, detail_blocks):
    shape = query.shape
    channels = shape[2]
    planes = lax.axis_size("z")
    cols = lax.axis_size("c")
    peers = ROWS * cols
    heads = HEADS // peers
    ch = heads * HEAD_DIM
    chp = -(-ch // 16) * 16
    plane = ("x", "c")
    my_z = lax.axis_index("z")
    my_col = lax.axis_index("c")
    me = lax.axis_index("x") * cols + my_col

    def flat(x):
        return x.reshape(LANES, channels)

    def swap(x):
        out = lax.all_to_all(x.reshape(peers, -1, LANES), plane, 0, 0, tiled=True)
        return out.reshape(x.shape)

    (sent,) = call(
        functools.partial(pack_body, ch),
        [((peers, 3, chp, LANES), BF)],
        flat(key), flat(value), flat(control),
        mib=56,
    )
    mine = swap(sent)
    wanted = lax.dynamic_index_in_dim(detail_blocks[0], my_col, 0, keepdims=False)
    named = (wanted >= 0) | (jnp.arange(cols) == my_col)
    named = jnp.concatenate([named, jnp.stack([my_z >= 1, my_z + 1 < planes])])
    live = jnp.where(jnp.pad(named, (0, 14 - cols)), 0.0, NEG).astype(F32)
    live = jnp.broadcast_to(live[:, None], (16, LANES))
    (sent_q,) = call(
        functools.partial(pack_live_body, ch, chp),
        [((peers, 2 * chp + 16, LANES), BF)],
        flat(query), flat(grad_out), live,
        mib=56,
    )
    down_pairs = [(i, i + 1) for i in range(planes - 1)]
    up_pairs = [(i + 1, i) for i in range(planes - 1)]
    mine, sent_q = lax.optimization_barrier((mine, sent_q))
    rim = (3 * cols + cols // 2, chp, LANES)
    to_up, to_down = call(rim_body, [(rim, BF)] * 2, mine)
    below = lax.ppermute(to_up, "z", up_pairs)
    above = lax.ppermute(to_down, "z", down_pairs)

    coefs = lax.dynamic_slice_in_dim(kernel.reshape(9, channels), me * ch, ch, 1)
    coefs = jnp.pad(coefs.T, ((0, chp - ch), (0, LANES - 9)))
    queries = swap(sent_q)

    wide = cols * LANES
    (values,) = call(
        values_body, [((ROWS + 2, chp, wide), BF)], mine, above, below, coefs, flops=4 * 10**9, keep=(0,)
    )
    side = (2 * cols + cols // 2, chp, LANES)
    flops = 10 * peers * heads * LANES * (wide + 2 * LANES) * 256
    dq, to_up, to_down, dk, dv = call(
        functools.partial(attend_body, heads),
        [
            ((peers, chp, LANES), BF),
            (side, BF),
            (side, BF),
            ((ROWS, chp, wide), F32),
            ((ROWS + 2, chp, wide), F32),
        ],
        queries, mine, above, below, values,
        scratch=[pltpu.VMEM((ROWS + 2, chp, wide), F32)],
        flops=flops,
        mib=6,
        near=(0, 1, 2, 3, 4),
        keep=(0, 1, 2, 3, 4),
    )
    from_below = lax.ppermute(to_up, "z", up_pairs)
    from_above = lax.ppermute(to_down, "z", down_pairs)

    blocks = -(-ch // LANES)
    (sent_dq,) = call(
        functools.partial(kernel_grad_body, ch),
        [((peers, chp + 32 * blocks, LANES), BF)],
        dq, mine, above, below, dv,
        scratch=[pltpu.VMEM((chp, LANES), F32)],
        flops=4 * 10**9,
    )
    dq_back = swap(sent_dq)

    (results,) = call(
        finish_body, [((peers, 3, chp, LANES), BF)], dk, dv, from_above, from_below, coefs,
        flops=4 * 10**9, near=(0, 1, 2, 3),
    )
    back = swap(results)
    grad_query, taps_sum = call(
        functools.partial(unpack_query_body, ch, chp),
        [((LANES, channels), BF), ((16, channels), F32)],
        dq_back,
    )
    step = 1
    while 2 * step < planes:
        other = lax.ppermute(taps_sum, "z", [(i, i ^ step) for i in range(planes)])
        (taps_sum,) = call(add_body, [((16, channels), F32)], taps_sum, other)
        step *= 2
    other = lax.ppermute(taps_sum, "z", [(i, i ^ step) for i in range(planes)])
    (grad_kernel,) = call(taps_out_body, [((3, 3, channels), F32)], taps_sum, other)
    outs = call(functools.partial(unpack_body, ch), [((LANES, channels), BF)] * 3, back)
    return tuple(x.reshape(shape) for x in [grad_query] + list(outs)) + (grad_kernel,)


def solution(mesh):
    trow, tcol = mesh.shape["trow"], mesh.shape["tcol"]
    grid = Mesh(mesh.devices.reshape(trow // ROWS, ROWS, tcol), ("z", "x", "c"))
    tiled = P(("z", "x"), "c", None)
    return jax.shard_map(
        per_device,
        mesh=grid,
        in_specs=(tiled, tiled, tiled, tiled, P(), tiled, P(("z", "x"), None, None)),
        out_specs=(tiled, tiled, tiled, tiled, P()),
        check_vma=False,
    )
```

```python
import functools
import math

import jax
import jax.numpy as jnp
from jax import lax
from jax.experimental import pallas as pl
from jax.experimental.pallas import tpu as pltpu
from jax.sharding import Mesh, PartitionSpec as P

HEADS = 16
HEAD_DIM = 72
ROWS = 2
LANES = 128
HALF = 64
NEG = -1e30
INV_ROOT = HEAD_DIM ** (-0.5)
LOG2E = 1.4426950408889634
BF = jnp.bfloat16
F32 = jnp.float32


def params(mib):
    return pltpu.CompilerParams(vmem_limit_bytes=mib << 20)


ANY = pl.BlockSpec(memory_space=pl.ANY)
VMEM = pl.BlockSpec(memory_space=pltpu.VMEM)


def call(body, outs, *args, scratch=(), flops=0, mib=8, aliases=None, far_in=(), far_out=(), hbm=()):
    moved = sum(a.size * a.dtype.itemsize for a in args)
    moved += sum(math.prod(shape) * jnp.dtype(dtype).itemsize for shape, dtype in outs)
    return pl.pallas_call(
        body,
        out_shape=[
            pltpu.HBM(shape, dtype) if n in hbm else jax.ShapeDtypeStruct(shape, dtype)
            for n, (shape, dtype) in enumerate(outs)
        ],
        in_specs=[ANY if n in far_in else VMEM for n in range(len(args))],
        out_specs=[ANY if n in far_out else VMEM for n in range(len(outs))],
        scratch_shapes=list(scratch),
        input_output_aliases=aliases or {},
        compiler_params=params(mib),
        cost_estimate=pl.CostEstimate(flops=flops, bytes_accessed=moved, transcendentals=0),
    )(*args)


def my_halves():
    odd = lax.rem(lax.axis_index("c"), 2)
    return [pl.ds(pl.multiple_of(x * HALF, HALF), HALF) for x in (odd, 1 - odd)]


def store_halves(out, x):
    for i, half in enumerate(my_halves()):
        out[half] = x[i * HALF : (i + 1) * HALF]


def pack_body(parts, ch, chp, *refs):
    ins = refs[:parts]
    live, out = refs[parts:-4], refs[-4]
    held, packed, sems = refs[-3:]
    halves = my_halves()

    def get(n):
        return [
            pltpu.make_async_copy(
                ins[n].at[halves[i]], held.at[n, pl.ds(i * HALF, HALF)], sems.at[i, n]
            )
            for i in range(2)
        ]

    for n in range(parts):
        for copy in get(n):
            copy.start()
    backs = []
    for n in range(parts):
        for copy in get(n):
            copy.wait()
        x = held[n]
        if ch % 16:
            x = x.astype(F32)
        x = x.T
        rows = pl.ds(n * chp, chp)
        for p in range(out.shape[0]):
            piece = x[p * ch : (p + 1) * ch]
            if chp > ch:
                piece = jnp.concatenate([piece, jnp.zeros((chp - ch, LANES), piece.dtype)], axis=0)
            packed[p, n * chp : (n + 1) * chp] = piece.astype(BF)
        if n == parts - 1 and live:
            for p in range(out.shape[0]):
                packed[p, parts * chp :] = live[0][...].astype(BF)
            rows = pl.ds(n * chp, chp + 16)
        backs.append(pltpu.make_async_copy(packed.at[:, rows], out.at[:, rows], sems.at[2, n]))
        backs[n].start()
    for back in backs:
        back.wait()


def unpack_body(ch, x_ref, *outs):
    peers = x_ref.shape[0]
    for n, out in enumerate(outs):
        pieces = [x_ref[p, n] for p in range(peers)]
        if ch % 16:
            pieces = [piece.astype(F32)[:ch] for piece in pieces]
        store_halves(out, jnp.concatenate(pieces, axis=0).T.astype(BF))


def unpack_query_body(ch, chp, x_ref, out, gk_ref):
    peers = x_ref.shape[0]
    pieces = [x_ref[p, :chp] for p in range(peers)]
    if ch % 16:
        pieces = [piece.astype(F32)[:ch] for piece in pieces]
    store_halves(out, jnp.concatenate(pieces, axis=0).T.astype(BF))
    blocks = (x_ref.shape[1] - chp) // 32
    wide = gk_ref.shape[1]
    total = [jnp.zeros((16, LANES), F32) for _ in range(wide // LANES + 2)]
    lane = lax.broadcasted_iota(jnp.int32, (16, LANES), 1)
    for p in range(peers):
        first, off = divmod(p * ch, LANES)
        for b in range(blocks):
            at = chp + 32 * b
            piece = x_ref[p, at : at + 16].astype(F32) + x_ref[p, at + 16 : at + 32].astype(F32)
            turned = pltpu.roll(piece, off, 1) if off else piece
            total[first + b] = total[first + b] + jnp.where(lane >= off, turned, 0.0)
            if off:
                total[first + b + 1] = total[first + b + 1] + jnp.where(lane < off, turned, 0.0)
    gk_ref[...] = jnp.concatenate(total[: wide // LANES], axis=1)


def taps_out_body(x_ref, y_ref, out):
    total = x_ref[...] + y_ref[...]
    for a in range(3):
        out[a] = total[3 * a : 3 * a + 3]


def add_body(x_ref, y_ref, out):
    out[...] = x_ref[...] + y_ref[...]


def second_rows(rows):
    lane = lax.broadcasted_iota(jnp.int32, (rows, LANES), 1)
    return lane >= HALF, lane < HALF


def lane_masks(rows):
    col = lax.broadcasted_iota(jnp.int32, (rows, LANES), 1) & (HALF - 1)
    return second_rows(rows), col == 0, col == HALF - 1


def col_shifts(tiles, masks):
    _, first, last = masks
    none = jnp.zeros_like(tiles[0])
    out = []
    for j, t in enumerate(tiles):
        before = tiles[j - 1] if j else none
        after = tiles[j + 1] if j + 1 < len(tiles) else none
        out.append(
            (
                pltpu.roll(jnp.where(last, before, t), 1, 1),
                t,
                pltpu.roll(jnp.where(first, after, t), LANES - 1, 1),
            )
        )
    return out


def conv_rows(rows, coef, masks):
    second = masks[0]
    count = len(rows)
    out = []
    last = None
    for i in range(count):
        here = []
        for j, t in enumerate(col_shifts(rows[i], masks)):
            use = [i < count - 1, 0 < i < count - 1, i > 0]
            here.append(
                [
                    coef[3 * a] * t[0] + coef[3 * a + 1] * t[1] + coef[3 * a + 2] * t[2] if use[a] else None
                    for a in range(3)
                ]
            )
        if i >= 2:
            out.append(
                [
                    m + pltpu.roll(u + jnp.where(second[j % 2], d, n[2]), HALF, 1)
                    for j, ((m, u, d), n) in enumerate(zip(last, here))
                ]
            )
        if 0 < i < count - 1:
            last = [
                (n[1], jnp.where(second[j % 2], p, n[0]), n[2])
                for j, (p, n) in enumerate(zip(before, here))
            ]
        before = [n[0] for n in here]
    return out


def taps(kc_ref, at):
    block = kc_ref[at, :]
    return [jnp.broadcast_to(block[:, t : t + 1], (16, LANES)) for t in range(9)]


def rim_body(a_ref, up_ref, down_ref):
    cols = a_ref.shape[0] // ROWS
    second = second_rows(a_ref.shape[2])
    for out, row, further, want in ((up_ref, 0, 1, 0), (down_ref, ROWS - 1, ROWS - 2, 1)):
        for j in range(cols):
            for n in range(3):
                out[n * cols + j] = a_ref[row * cols + j, n]
        for m in range(0, cols, 2):
            even, odd = (a_ref[further * cols + m + i, 2].astype(F32) for i in range(2))
            out[3 * cols + m // 2] = jnp.where(second[want], odd, even).astype(BF)


def control_rows(a_ref, u_ref, d_ref, at):
    cols = a_ref.shape[0] // ROWS
    rows = [
        [u_ref[3 * cols + j // 2, at, :] for j in range(cols)],
        [u_ref[2 * cols + j, at, :] for j in range(cols)],
        *[[a_ref[r * cols + j, 2, at, :] for j in range(cols)] for r in range(ROWS)],
        [d_ref[2 * cols + j, at, :] for j in range(cols)],
        [d_ref[3 * cols + j // 2, at, :] for j in range(cols)],
    ]
    return [[x.astype(F32) for x in row] for row in rows]


def values_body(a_ref, u_ref, d_ref, kc_ref, a_out, u_out, d_out):
    cols = a_ref.shape[0] // ROWS
    chp = a_ref.shape[2]

    @pl.loop(0, chp // 16)
    def _(step):
        at = pl.ds(pl.multiple_of(step * 16, 16), 16)
        conv = conv_rows(control_rows(a_ref, u_ref, d_ref, at), taps(kc_ref, at), lane_masks(16))
        for ref, out in ((u_ref, u_out), (d_ref, d_out)):
            for n in range(ref.shape[0]):
                if not cols <= n < 2 * cols:
                    out[n, at, :] = ref[n, at, :]
        for j in range(cols):
            for ref, out, i in ((u_ref, u_out, 0), (d_ref, d_out, -1)):
                out[cols + j, at, :] = (ref[cols + j, at, :].astype(F32) + conv[i][j]).astype(BF)
            for r in range(ROWS):
                tile = r * cols + j
                a_out[tile, 0, at, :] = a_ref[tile, 0, at, :]
                a_out[tile, 1, at, :] = (a_ref[tile, 1, at, :].astype(F32) + conv[r + 1][j]).astype(BF)
                a_out[tile, 2, at, :] = a_ref[tile, 2, at, :]


def attend_body(heads, q_ref, a_ref, u_ref, d_ref, dq_ref, up_ref, down_ref, dk_ref, dv_ref):
    peers = q_ref.shape[0]
    cols = peers // ROWS
    chp = a_ref.shape[2]
    wide = cols * LANES

    dk_ref[...] = jnp.zeros_like(dk_ref)
    dv_ref[...] = jnp.zeros_like(dv_ref)
    chan = lax.broadcasted_iota(jnp.int32, (chp, LANES), 0)
    mine = [(chan >= h * HEAD_DIM) & (chan < (h + 1) * HEAD_DIM) for h in range(heads)]

    def spread(x):
        x = x.astype(F32)
        return jnp.concatenate([jnp.where(m, x, 0.0) for m in mine], axis=1).astype(BF)

    def dot(x, y, on_x, on_y):
        return lax.dot_general(
            x, y, (((on_x,), (on_y,)), ((), ())), preferred_element_type=F32
        )

    for r in range(ROWS):

        for j in range(cols):
            tile = r * cols + j
            span = slice(j * LANES, (j + 1) * LANES)
            q = spread(q_ref[tile, :chp])
            g = spread(q_ref[tile, chp : 2 * chp])

            def all_keys(n):
                above = u_ref[n * cols + j] if r == 0 else a_ref[tile - cols, n]
                below = d_ref[n * cols + j] if r == ROWS - 1 else a_ref[tile + cols, n]
                row = [a_ref[r * cols + p, n] for p in range(cols)]
                return jnp.concatenate(row + [above, below], axis=1)

            k = all_keys(0)
            v = all_keys(1)
            live = q_ref[tile, 2 * chp :].astype(F32)
            zero = jnp.zeros((1, LANES), F32)
            bias = jnp.concatenate(
                [live[p : p + 1] for p in range(cols)]
                + [
                    live[cols : cols + 1] if r == 0 else zero,
                    live[cols + 1 : cols + 2] if r == ROWS - 1 else zero,
                ],
                axis=1,
            )
            s = dot(q, k, 0, 0) + bias
            top = jnp.max(s, axis=1, keepdims=True)
            e = jnp.exp2((s - top) * (INV_ROOT * LOG2E))
            w = e * (1.0 / jnp.sum(e, axis=1, keepdims=True))
            gw = dot(g, v, 0, 0)
            delta = jnp.sum(w * gw, axis=1, keepdims=True)
            gs = (w * (gw - delta)).astype(BF)
            dk = dot(q, gs, 1, 0)
            dv = dot(g, w.astype(BF), 1, 0)
            dq = dot(k, gs, 1, 1)
            own = dq[:, :LANES]
            for h in range(1, heads):
                own = jnp.where(mine[h], dq[:, h * LANES : (h + 1) * LANES], own)
            dq_ref[tile] = (own * INV_ROOT).astype(BF)
            dk_ref[r] += dk[:, :wide]
            dv_ref[r] += dv[:, :wide]
            for side, at in ((r - 1, wide), (r + 1, wide + LANES)):
                dk_side, dv_side = dk[:, at : at + LANES], dv[:, at : at + LANES]
                if 0 <= side < ROWS:
                    dk_ref[side, :, span] += dk_side
                    dv_ref[side, :, span] += dv_side
                else:
                    out = up_ref if side < 0 else down_ref
                    out[j] = (dk_side * INV_ROOT).astype(BF)
                    out[cols + j] = dv_side.astype(BF)

    second = second_rows(chp)
    for out, row, want in ((up_ref, 0, 0), (down_ref, ROWS - 1, 1)):
        for m in range(0, cols, 2):
            even, odd = (dv_ref[row, :, (m + i) * LANES : (m + i + 1) * LANES] for i in range(2))
            out[2 * cols + m // 2] = jnp.where(second[1 - want], even, odd).astype(BF)


def value_terms(dv_ref, up_ref, down_ref, i, j, at):
    cols = dv_ref.shape[2] // LANES
    if i == 0:
        return up_ref[cols + j, at, :].astype(F32)
    if i == ROWS + 1:
        return down_ref[cols + j, at, :].astype(F32)
    return dv_ref[i - 1, at, j * LANES : (j + 1) * LANES]


def kernel_grad_body(
    ch, dq_ref, a_ref, u_ref, d_ref, dk_ref, dv_ref, up_ref, down_ref, out_ref, dk_out, dv_out, sums, rows, sems
):
    cols = dv_ref.shape[2] // LANES
    chp = dv_ref.shape[1]
    copies = [
        pltpu.make_async_copy(dq_ref, out_ref.at[:, pl.ds(0, chp)], sems.at[0]),
        pltpu.make_async_copy(dk_ref, dk_out, sems.at[1]),
        pltpu.make_async_copy(dv_ref, dv_out, sems.at[2]),
    ]
    for copy in copies:
        copy.start()

    @pl.loop(0, chp // 16)
    def _(step):
        at = pl.ds(pl.multiple_of(step * 16, 16), 16)
        masks = lane_masks(16)
        second = masks[0]
        acc = [jnp.zeros((16, LANES), F32) for _ in range(9)]
        above = here = None
        for i, row in enumerate(control_rows(a_ref, u_ref, d_ref, at)):
            below = col_shifts(row, masks)
            if i >= 2:
                for j in range(cols):
                    g = value_terms(dv_ref, up_ref, down_ref, i - 2, j, at)
                    turned = pltpu.roll(g, HALF, 1)
                    for b in range(3):
                        acc[b] += jnp.where(second[j % 2], above[j][b], here[j][b]) * turned
                        acc[3 + b] += here[j][b] * g
                        acc[6 + b] += jnp.where(second[j % 2], here[j][b], below[j][b]) * turned
            above, here = here, below
        lane = lax.broadcasted_iota(jnp.int32, (16, LANES), 1)
        out = jnp.zeros((16, LANES), F32)
        for t in range(9):
            out = jnp.where(lane == t, jnp.sum(acc[t], axis=1, keepdims=True), out)
        sums[at, :] = out

    turned = sums[...].T[:16]
    blocks = rows.shape[1] // 32
    if blocks * LANES > chp:
        turned = jnp.concatenate([turned, jnp.zeros((16, blocks * LANES - chp), F32)], axis=1)
    lane = lax.broadcasted_iota(jnp.int32, turned.shape, 1)
    turned = jnp.where(lane < ch, turned, 0.0)
    high = turned.astype(BF)
    low = (turned - high.astype(F32)).astype(BF)
    for tile in range(rows.shape[0]):
        for b in range(blocks):
            rows[tile, 32 * b : 32 * b + 16] = high[:, b * LANES : (b + 1) * LANES]
            rows[tile, 32 * b + 16 : 32 * b + 32] = low[:, b * LANES : (b + 1) * LANES]
    sums_out = pltpu.make_async_copy(rows, out_ref.at[:, pl.ds(chp, 32 * blocks)], sems.at[3])
    sums_out.start()
    for copy in copies + [sums_out]:
        copy.wait()


def finish_body(
    dk_hbm, dv_hbm, up_ref, down_ref, u_ref, d_ref, kc_ref, out_ref, dk_ref, dv_ref, held, sems
):
    cols = held.shape[0] // ROWS
    chp = held.shape[2]

    def chunk(step):
        return pl.ds(pl.multiple_of(step * 16, 16), 16)

    def get(step):
        at = chunk(step)
        return [
            pltpu.make_async_copy(dk_hbm.at[:, at], dk_ref.at[:, at], sems.at[0, step]),
            pltpu.make_async_copy(dv_hbm.at[:, at], dv_ref.at[:, at], sems.at[1, step]),
        ]

    def put(step):
        at = chunk(step)
        return pltpu.make_async_copy(held.at[:, :, at], out_ref.at[:, :, at], sems.at[2, step])

    @pl.loop(0, chp // 16)
    def _(step):
        for copy in get(step):
            copy.start()

    @pl.loop(0, chp // 16)
    def _(step):
        for copy in get(step):
            copy.wait()
        at = chunk(step)
        masks = lane_masks(16)
        coef = taps(kc_ref, at)[::-1]

        def from_side(ref, n):
            return ref[n, at, :].astype(F32)

        def rounded(x):
            return x.astype(BF).astype(F32)

        rows = []
        for i in range(ROWS + 2):
            row = []
            for j in range(cols):
                x = value_terms(dv_ref, up_ref, down_ref, i, j, at)
                if i == 0:
                    rim = from_side(u_ref, 2 * cols + j // 2)
                    x = x + rim
                elif i == ROWS + 1:
                    rim = from_side(d_ref, 2 * cols + j // 2)
                    x = x + rim
                else:
                    if i == 1:
                        x = x + from_side(u_ref, cols + j)
                    if i == ROWS:
                        x = x + from_side(d_ref, cols + j)
                row.append(rounded(x))
            rows.append(row)
        conv = conv_rows(rows, coef, masks)
        for r in range(ROWS):
            for j in range(cols):
                tile = r * cols + j
                k = dk_ref[r, at, j * LANES : (j + 1) * LANES] * INV_ROOT
                if r == 0:
                    k = k + from_side(u_ref, j)
                if r == ROWS - 1:
                    k = k + from_side(d_ref, j)
                held[tile, 0, at, :] = k.astype(BF)
                held[tile, 1, at, :] = rows[r + 1][j].astype(BF)
                held[tile, 2, at, :] = conv[r][j].astype(BF)
        put(step).start()

    @pl.loop(0, chp // 16)
    def _(step):
        put(step).wait()


def per_device(query, key, value, control, kernel, grad_out, detail_blocks):
    shape = query.shape
    channels = shape[2]
    planes = lax.axis_size("z")
    cols = lax.axis_size("c")
    peers = ROWS * cols
    heads = HEADS // peers
    ch = heads * HEAD_DIM
    chp = -(-ch // 16) * 16
    plane = ("x", "c")
    my_z = lax.axis_index("z")
    my_col = lax.axis_index("c")
    me = lax.axis_index("x") * cols + my_col

    def flat(x):
        return x.reshape(LANES, channels)

    def swap(x):
        return lax.all_to_all(x.reshape(peers, -1, LANES), plane, 0, 0, tiled=True)

    def pack(arrays, *live):
        parts = len(arrays)
        rows = parts * chp + 16 * len(live)
        (out,) = call(
            functools.partial(pack_body, parts, ch, chp),
            [((peers, rows, LANES), BF)],
            *[flat(x) for x in arrays], *live,
            scratch=[
                pltpu.VMEM((parts, LANES, channels), BF),
                pltpu.VMEM((peers, rows, LANES), BF),
                pltpu.SemaphoreType.DMA((3, parts)),
            ],
            mib=56,
            far_in=range(parts),
            far_out=(0,),
        )
        return out

    sent = pack([key, value, control])
    mine = swap(sent).reshape(peers, 3, chp, LANES)
    wanted = lax.dynamic_index_in_dim(detail_blocks[0], my_col, 0, keepdims=False)
    named = (wanted >= 0) | (jnp.arange(cols) == my_col)
    named = jnp.concatenate([named, jnp.stack([my_z >= 1, my_z + 1 < planes])])
    live = jnp.where(jnp.pad(named, (0, 14 - cols)), 0.0, NEG).astype(F32)
    live = jnp.broadcast_to(live[:, None], (16, LANES))
    sent_q = pack([query, grad_out], live)
    mine, sent_q = lax.optimization_barrier((mine, sent_q))
    down_pairs = [(i, i + 1) for i in range(planes - 1)]
    up_pairs = [(i + 1, i) for i in range(planes - 1)]
    rim = (3 * cols + cols // 2, chp, LANES)
    to_up, to_down = call(rim_body, [(rim, BF)] * 2, mine)
    below = lax.ppermute(to_up, "z", up_pairs)
    above = lax.ppermute(to_down, "z", down_pairs)

    coefs = lax.dynamic_slice_in_dim(kernel.reshape(9, channels), me * ch, ch, 1)
    coefs = jnp.pad(coefs.T, ((0, chp - ch), (0, LANES - 9)))
    queries = swap(sent_q)

    wide = cols * LANES

    def tiles(*lead):
        return lead + (chp, LANES), BF

    mine, above, below = call(
        values_body,
        [(x.shape, BF) for x in (mine, above, below)],
        mine, above, below, coefs,
        flops=4 * 10**9,
        aliases={0: 0, 1: 1, 2: 2},
    )
    side = (2 * cols + cols // 2, chp, LANES)
    flops = 10 * peers * heads * LANES * (wide + 2 * LANES) * 256
    dq, to_up, to_down, dk, dv = call(
        functools.partial(attend_body, heads),
        [
            ((peers, chp, LANES), BF),
            (side, BF),
            (side, BF),
            ((ROWS, chp, wide), F32),
            ((ROWS, chp, wide), F32),
        ],
        queries, mine, above, below,
        flops=flops,
        mib=6,
    )
    from_above = lax.ppermute(to_down, "z", down_pairs)
    from_below = lax.ppermute(to_up, "z", up_pairs)

    blocks = -(-ch // LANES)
    own = ((ROWS, chp, wide), F32)
    sent_dq, dk, dv = call(
        functools.partial(kernel_grad_body, ch),
        [((peers, chp + 32 * blocks, LANES), BF), own, own],
        dq, mine, above, below, dk, dv, to_up, to_down,
        scratch=[
            pltpu.VMEM((chp, LANES), F32),
            pltpu.VMEM((peers, 32 * blocks, LANES), BF),
            pltpu.SemaphoreType.DMA((4,)),
        ],
        far_out=(0, 1, 2),
        hbm=(1, 2),
        flops=4 * 10**9,
    )
    dq_back = swap(sent_dq)

    (results,) = call(
        finish_body, [tiles(peers, 3)],
        *[pltpu.with_memory_space_constraint(x, pltpu.HBM) for x in (dk, dv)],
        to_up, to_down, from_above, from_below, coefs,
        scratch=[
            pltpu.VMEM((ROWS, chp, wide), F32),
            pltpu.VMEM((ROWS, chp, wide), F32),
            pltpu.VMEM((peers, 3, chp, LANES), BF),
            pltpu.SemaphoreType.DMA((3, chp // 16)),
        ],
        far_in=(0, 1),
        far_out=(0,),
        flops=4 * 10**9,
    )
    back = swap(results).reshape(peers, 3, chp, LANES)
    grad_query, taps_sum = call(
        functools.partial(unpack_query_body, ch, chp),
        [((LANES, channels), BF), ((16, channels), F32)],
        dq_back,
    )
    step = 1
    while 2 * step < planes:
        other = lax.ppermute(taps_sum, "z", [(i, i ^ step) for i in range(planes)])
        (taps_sum,) = call(add_body, [((16, channels), F32)], taps_sum, other)
        step *= 2
    other = lax.ppermute(taps_sum, "z", [(i, i ^ step) for i in range(planes)])
    (grad_kernel,) = call(taps_out_body, [((3, 3, channels), F32)], taps_sum, other)
    outs = call(functools.partial(unpack_body, ch), [((LANES, channels), BF)] * 3, back)
    return tuple(x.reshape(shape) for x in [grad_query] + list(outs)) + (grad_kernel,)


def solution(mesh):
    trow, tcol = mesh.shape["trow"], mesh.shape["tcol"]
    grid = Mesh(mesh.devices.reshape(trow // ROWS, ROWS, tcol), ("z", "x", "c"))
    tiled = P(("z", "x"), "c", None)
    return jax.shard_map(
        per_device,
        mesh=grid,
        in_specs=(tiled, tiled, tiled, tiled, P(), tiled, P(("z", "x"), None, None)),
        out_specs=(tiled, tiled, tiled, tiled, P()),
        check_vma=False,
    )
```

```python
import functools
import math

import jax
import jax.numpy as jnp
from jax import lax
from jax.experimental import pallas as pl
from jax.experimental.pallas import tpu as pltpu
from jax.sharding import Mesh, PartitionSpec as P

HEADS = 16
HEAD_DIM = 72
ROWS = 2
LANES = 128
HALF = 64
NEG = -1e30
INV_ROOT = HEAD_DIM ** (-0.5)
LOG2E = 1.4426950408889634
BF = jnp.bfloat16
F32 = jnp.float32


def params(mib):
    return pltpu.CompilerParams(vmem_limit_bytes=mib << 20)


ANY = pl.BlockSpec(memory_space=pl.ANY)
VMEM = pl.BlockSpec(memory_space=pltpu.VMEM)


def call(body, outs, *args, scratch=(), flops=0, mib=8, aliases=None, far_in=(), far_out=(), hbm=()):
    moved = sum(a.size * a.dtype.itemsize for a in args)
    moved += sum(math.prod(shape) * jnp.dtype(dtype).itemsize for shape, dtype in outs)
    return pl.pallas_call(
        body,
        out_shape=[
            (pltpu.HBM if n in hbm else jax.ShapeDtypeStruct)(shape, dtype)
            for n, (shape, dtype) in enumerate(outs)
        ],
        in_specs=[ANY if n in far_in else VMEM for n in range(len(args))],
        out_specs=[ANY if n in far_out else VMEM for n in range(len(outs))],
        scratch_shapes=list(scratch),
        input_output_aliases=aliases or {},
        compiler_params=params(mib),
        cost_estimate=pl.CostEstimate(flops=flops, bytes_accessed=moved, transcendentals=0),
    )(*args)


def my_halves():
    odd = lax.rem(lax.axis_index("c"), 2)
    return [pl.ds(pl.multiple_of(x * HALF, HALF), HALF) for x in (odd, 1 - odd)]


def store_halves(out, x):
    for i, half in enumerate(my_halves()):
        out[half] = x[i * HALF : (i + 1) * HALF]


def pack_body(parts, ch, chp, *refs):
    ins = refs[:parts]
    live, out = refs[parts:-4], refs[-4]
    held, packed, sems = refs[-3:]
    halves = my_halves()

    def get(n):
        return [
            pltpu.make_async_copy(
                ins[n].at[halves[i]], held.at[n, pl.ds(i * HALF, HALF)], sems.at[i, n]
            )
            for i in range(2)
        ]

    for n in range(parts):
        for copy in get(n):
            copy.start()
    backs = []
    for n in range(parts):
        for copy in get(n):
            copy.wait()
        x = held[n]
        if ch % 16:
            x = x.astype(F32)
        x = x.T
        rows = pl.ds(n * chp, chp)
        for p in range(out.shape[0]):
            piece = x[p * ch : (p + 1) * ch]
            if chp > ch:
                piece = jnp.concatenate([piece, jnp.zeros((chp - ch, LANES), piece.dtype)], axis=0)
            packed[p, n * chp : (n + 1) * chp] = piece.astype(BF)
        if n == parts - 1 and live:
            for p in range(out.shape[0]):
                packed[p, parts * chp :] = live[0][...].astype(BF)
            rows = pl.ds(n * chp, chp + 16)
        backs.append(pltpu.make_async_copy(packed.at[:, rows], out.at[:, rows], sems.at[2, n]))
        backs[n].start()
    for back in backs:
        back.wait()


def unpack_body(ch, x_ref, *outs):
    peers = x_ref.shape[0]
    for n, out in enumerate(outs):
        pieces = [x_ref[p, n] for p in range(peers)]
        if ch % 16:
            pieces = [piece.astype(F32)[:ch] for piece in pieces]
        store_halves(out, jnp.concatenate(pieces, axis=0).T.astype(BF))


def unpack_query_body(ch, chp, x_ref, out, gk_ref):
    peers = x_ref.shape[0]
    pieces = [x_ref[p, :chp] for p in range(peers)]
    if ch % 16:
        pieces = [piece.astype(F32)[:ch] for piece in pieces]
    store_halves(out, jnp.concatenate(pieces, axis=0).T.astype(BF))
    wide = gk_ref.shape[1]
    total = [jnp.zeros((16, LANES), F32) for _ in range(wide // LANES + 2)]
    lane = lax.broadcasted_iota(jnp.int32, (16, LANES), 1)
    for p in range(peers):
        table = x_ref[p, chp:].astype(F32)
        pieces = [table[:16] + pltpu.roll(table, 32 - 9, 0)[:16]]
        if ch > LANES:
            more = pltpu.roll(table, 32 - 18, 0)[:16]
            more = more + pltpu.roll(more, 2 * LANES - ch, 1)
            pieces.append(jnp.where(lane < ch - LANES, more, 0.0))
        first, off = divmod(p * ch, LANES)
        for b, piece in enumerate(pieces):
            turned = pltpu.roll(piece, off, 1) if off else piece
            total[first + b] = total[first + b] + jnp.where(lane >= off, turned, 0.0)
            if off:
                total[first + b + 1] = total[first + b + 1] + jnp.where(lane < off, turned, 0.0)
    gk_ref[...] = jnp.concatenate(total[: wide // LANES], axis=1)


def taps_out_body(x_ref, y_ref, out):
    total = x_ref[...] + y_ref[...]
    for a in range(3):
        out[a] = total[3 * a : 3 * a + 3]


def add_body(x_ref, y_ref, out):
    out[...] = x_ref[...] + y_ref[...]


def second_rows(rows):
    lane = lax.broadcasted_iota(jnp.int32, (rows, LANES), 1)
    return lane >= HALF, lane < HALF


def lane_masks(rows):
    col = lax.broadcasted_iota(jnp.int32, (rows, LANES), 1) & (HALF - 1)
    return second_rows(rows), col == 0, col == HALF - 1


def col_shifts(tiles, masks):
    _, first, last = masks
    none = jnp.zeros_like(tiles[0])
    out = []
    for j, t in enumerate(tiles):
        before = tiles[j - 1] if j else none
        after = tiles[j + 1] if j + 1 < len(tiles) else none
        out.append(
            (
                pltpu.roll(jnp.where(last, before, t), 1, 1),
                t,
                pltpu.roll(jnp.where(first, after, t), LANES - 1, 1),
            )
        )
    return out


def conv_rows(rows, coef, masks):
    second = masks[0]
    count = len(rows)
    out = []
    last = None
    for i in range(count):
        here = []
        for j, t in enumerate(col_shifts(rows[i], masks)):
            use = [i < count - 1, 0 < i < count - 1, i > 0]
            here.append(
                [
                    coef[3 * a] * t[0] + coef[3 * a + 1] * t[1] + coef[3 * a + 2] * t[2] if use[a] else None
                    for a in range(3)
                ]
            )
        if i >= 2:
            out.append(
                [
                    m + pltpu.roll(u + jnp.where(second[j % 2], d, n[2]), HALF, 1)
                    for j, ((m, u, d), n) in enumerate(zip(last, here))
                ]
            )
        if 0 < i < count - 1:
            last = [
                (n[1], jnp.where(second[j % 2], p, n[0]), n[2])
                for j, (p, n) in enumerate(zip(before, here))
            ]
        before = [n[0] for n in here]
    return out


def taps(kc_ref, at):
    block = kc_ref[at, :]
    return [jnp.broadcast_to(block[:, t : t + 1], (16, LANES)) for t in range(9)]


def rim_body(a_ref, up_ref, down_ref):
    cols = a_ref.shape[0] // ROWS
    second = second_rows(a_ref.shape[2])
    for out, row, further, want in ((up_ref, 0, 1, 0), (down_ref, ROWS - 1, ROWS - 2, 1)):
        for j in range(cols):
            for n in range(3):
                out[n * cols + j] = a_ref[row * cols + j, n]
        for m in range(0, cols, 2):
            even, odd = (a_ref[further * cols + m + i, 2].astype(F32) for i in range(2))
            out[3 * cols + m // 2] = jnp.where(second[want], odd, even).astype(BF)


def control_rows(a_ref, u_ref, d_ref, at):
    cols = a_ref.shape[0] // ROWS
    rows = [
        [u_ref[3 * cols + j // 2, at, :] for j in range(cols)],
        [u_ref[2 * cols + j, at, :] for j in range(cols)],
        *[[a_ref[r * cols + j, 2, at, :] for j in range(cols)] for r in range(ROWS)],
        [d_ref[2 * cols + j, at, :] for j in range(cols)],
        [d_ref[3 * cols + j // 2, at, :] for j in range(cols)],
    ]
    return [[x.astype(F32) for x in row] for row in rows]


def values_body(a_ref, u_ref, d_ref, kc_ref, a_out, u_out, d_out):
    cols = a_ref.shape[0] // ROWS
    chp = a_ref.shape[2]

    @pl.loop(0, chp // 16)
    def _(step):
        at = pl.ds(pl.multiple_of(step * 16, 16), 16)
        conv = conv_rows(control_rows(a_ref, u_ref, d_ref, at), taps(kc_ref, at), lane_masks(16))
        for ref, out in ((u_ref, u_out), (d_ref, d_out)):
            for n in range(ref.shape[0]):
                if not cols <= n < 2 * cols:
                    out[n, at, :] = ref[n, at, :]
        for j in range(cols):
            for ref, out, i in ((u_ref, u_out, 0), (d_ref, d_out, -1)):
                out[cols + j, at, :] = (ref[cols + j, at, :].astype(F32) + conv[i][j]).astype(BF)
            for r in range(ROWS):
                tile = r * cols + j
                a_out[tile, 0, at, :] = a_ref[tile, 0, at, :]
                a_out[tile, 1, at, :] = (a_ref[tile, 1, at, :].astype(F32) + conv[r + 1][j]).astype(BF)
                a_out[tile, 2, at, :] = a_ref[tile, 2, at, :]


def attend_body(heads, q_ref, a_ref, u_ref, d_ref, dq_ref, up_ref, down_ref, dk_ref, dv_ref):
    peers = q_ref.shape[0]
    cols = peers // ROWS
    chp = a_ref.shape[2]
    wide = cols * LANES

    dk_ref[...] = jnp.zeros_like(dk_ref)
    dv_ref[...] = jnp.zeros_like(dv_ref)
    chan = lax.broadcasted_iota(jnp.int32, (chp, LANES), 0)
    mine = [(chan >= h * HEAD_DIM) & (chan < (h + 1) * HEAD_DIM) for h in range(heads)]

    def spread(x):
        x = x.astype(F32)
        return jnp.concatenate([jnp.where(m, x, 0.0) for m in mine], axis=1).astype(BF)

    def dot(x, y, on_x, on_y):
        return lax.dot_general(
            x, y, (((on_x,), (on_y,)), ((), ())), preferred_element_type=F32
        )

    def front(tile):
        r, j = divmod(tile, cols)
        q = spread(q_ref[tile, :chp])
        g = spread(q_ref[tile, chp : 2 * chp])

        def all_keys(n):
            above = u_ref[n * cols + j] if r == 0 else a_ref[tile - cols, n]
            below = d_ref[n * cols + j] if r == ROWS - 1 else a_ref[tile + cols, n]
            row = [a_ref[r * cols + p, n] for p in range(cols)]
            return jnp.concatenate(row + [above, below], axis=1)

        k = all_keys(0)
        return q, g, k, dot(q, k, 0, 0), dot(g, all_keys(1), 0, 0)

    def middle(tile, s, gw):
        r = tile // cols
        live = q_ref[tile, 2 * chp :].astype(F32)
        zero = jnp.zeros((1, LANES), F32)
        bias = jnp.concatenate(
            [live[p : p + 1] for p in range(cols)]
            + [
                live[cols : cols + 1] if r == 0 else zero,
                live[cols + 1 : cols + 2] if r == ROWS - 1 else zero,
            ],
            axis=1,
        )
        s = s + bias
        top = jnp.max(s, axis=1, keepdims=True)
        e = jnp.exp2((s - top) * (INV_ROOT * LOG2E))
        w = e * (1.0 / jnp.sum(e, axis=1, keepdims=True))
        delta = jnp.sum(w * gw, axis=1, keepdims=True)
        return w.astype(BF), (w * (gw - delta)).astype(BF)

    def back(tile, q, g, k, w, gs):
        r, j = divmod(tile, cols)
        span = slice(j * LANES, (j + 1) * LANES)
        dk = dot(q, gs, 1, 0)
        dv = dot(g, w, 1, 0)
        dq = dot(k, gs, 1, 1)
        own = dq[:, :LANES]
        for h in range(1, heads):
            own = jnp.where(mine[h], dq[:, h * LANES : (h + 1) * LANES], own)
        dq_ref[tile] = (own * INV_ROOT).astype(BF)
        dk_ref[r] += dk[:, :wide]
        dv_ref[r] += dv[:, :wide]
        for side, at in ((r - 1, wide), (r + 1, wide + LANES)):
            dk_side, dv_side = dk[:, at : at + LANES], dv[:, at : at + LANES]
            if 0 <= side < ROWS:
                dk_ref[side, :, span] += dk_side
                dv_ref[side, :, span] += dv_side
            else:
                out = up_ref if side < 0 else down_ref
                out[j] = (dk_side * INV_ROOT).astype(BF)
                out[cols + j] = dv_side.astype(BF)

    ahead = front(0)
    for tile in range(peers):
        q, g, k, s, gw = ahead
        if tile + 1 < peers:
            ahead = front(tile + 1)
        halves = [middle(tile, s[i : i + 64], gw[i : i + 64]) for i in range(0, s.shape[0], 64)]
        w, gs = (jnp.concatenate(x, axis=0) for x in zip(*halves))
        back(tile, q, g, k, w, gs)

    second = second_rows(chp)
    for out, row, want in ((up_ref, 0, 0), (down_ref, ROWS - 1, 1)):
        for m in range(0, cols, 2):
            even, odd = (dv_ref[row, :, (m + i) * LANES : (m + i + 1) * LANES] for i in range(2))
            out[2 * cols + m // 2] = jnp.where(second[1 - want], even, odd).astype(BF)


def value_terms(dv_ref, up_ref, down_ref, i, j, at):
    cols = dv_ref.shape[2] // LANES
    if i == 0:
        return up_ref[cols + j, at, :].astype(F32)
    if i == ROWS + 1:
        return down_ref[cols + j, at, :].astype(F32)
    return dv_ref[i - 1, at, j * LANES : (j + 1) * LANES]


def kernel_grad_body(
    ch, dq_ref, a_ref, u_ref, d_ref, dk_ref, dv_ref, up_ref, down_ref, out_ref, dk_out, dv_out, sums, rows, sems
):
    cols = dv_ref.shape[2] // LANES
    chp = dv_ref.shape[1]
    copies = [
        pltpu.make_async_copy(dq_ref, out_ref.at[:, pl.ds(0, chp)], sems.at[0]),
        pltpu.make_async_copy(dk_ref, dk_out, sems.at[1]),
        pltpu.make_async_copy(dv_ref, dv_out, sems.at[2]),
    ]
    for copy in copies:
        copy.start()

    @pl.loop(0, chp // 16)
    def _(step):
        at = pl.ds(pl.multiple_of(step * 16, 16), 16)
        masks = lane_masks(16)
        second = masks[0]
        acc = [jnp.zeros((16, LANES), F32) for _ in range(9)]
        above = here = None
        for i, row in enumerate(control_rows(a_ref, u_ref, d_ref, at)):
            below = col_shifts(row, masks)
            if i >= 2:
                for j in range(cols):
                    g = value_terms(dv_ref, up_ref, down_ref, i - 2, j, at)
                    turned = pltpu.roll(g, HALF, 1)
                    for b in range(3):
                        acc[b] += jnp.where(second[j % 2], above[j][b], here[j][b]) * turned
                        acc[3 + b] += here[j][b] * g
                        acc[6 + b] += jnp.where(second[j % 2], here[j][b], below[j][b]) * turned
            above, here = here, below
        lane = lax.broadcasted_iota(jnp.int32, (16, LANES), 1)
        out = jnp.zeros((16, LANES), F32)
        for t in range(9):
            out = jnp.where(lane == t, jnp.sum(acc[t], axis=1, keepdims=True), out)
        sums[at, :] = out

    def split(x):
        high = x.astype(BF).astype(F32)
        return high, x - high

    high, low = split(sums[: min(chp, LANES)])
    table = high + pltpu.roll(low, 9, 1)
    if chp < LANES:
        table = jnp.concatenate([table, jnp.zeros((LANES - chp, LANES), F32)], axis=0)
    if chp > LANES:
        more = jnp.concatenate(split(sums[LANES:]), axis=0)
        more = jnp.concatenate([more, jnp.zeros((LANES - more.shape[0], LANES), F32)], axis=0)
        table = table + pltpu.roll(more, 18, 1)
    table = table.T[:32].astype(BF)
    for tile in range(rows.shape[0]):
        rows[tile] = table
    sums_out = pltpu.make_async_copy(rows, out_ref.at[:, pl.ds(chp, 32)], sems.at[3])
    sums_out.start()
    for copy in copies + [sums_out]:
        copy.wait()


def finish_body(
    dk_hbm, dv_hbm, up_ref, down_ref, d_ref, u_ref, kc_ref, out_ref, dk_ref, dv_ref, held, sems
):
    cols = held.shape[0] // ROWS
    chp = held.shape[2]

    def chunk(step):
        return pl.ds(pl.multiple_of(step * 16, 16), 16)

    def get(step):
        at = chunk(step)
        return [
            pltpu.make_async_copy(dk_hbm.at[:, at], dk_ref.at[:, at], sems.at[0, step]),
            pltpu.make_async_copy(dv_hbm.at[:, at], dv_ref.at[:, at], sems.at[1, step]),
        ]

    def put(step):
        at = chunk(step)
        return pltpu.make_async_copy(held.at[:, :, at], out_ref.at[:, :, at], sems.at[2, step])

    @pl.loop(0, chp // 16)
    def _(step):
        for copy in get(step):
            copy.start()

    @pl.loop(0, chp // 16)
    def _(step):
        for copy in get(step):
            copy.wait()
        at = chunk(step)
        masks = lane_masks(16)
        coef = taps(kc_ref, at)[::-1]

        def from_side(ref, n):
            return ref[n, at, :].astype(F32)

        def rounded(x):
            return x.astype(BF).astype(F32)

        rows = []
        for i in range(ROWS + 2):
            row = []
            for j in range(cols):
                x = value_terms(dv_ref, up_ref, down_ref, i, j, at)
                if i == 0:
                    rim = from_side(u_ref, 2 * cols + j // 2)
                    x = x + rim
                elif i == ROWS + 1:
                    rim = from_side(d_ref, 2 * cols + j // 2)
                    x = x + rim
                else:
                    if i == 1:
                        x = x + from_side(u_ref, cols + j)
                    if i == ROWS:
                        x = x + from_side(d_ref, cols + j)
                row.append(rounded(x))
            rows.append(row)
        conv = conv_rows(rows, coef, masks)
        for r in range(ROWS):
            for j in range(cols):
                tile = r * cols + j
                k = dk_ref[r, at, j * LANES : (j + 1) * LANES] * INV_ROOT
                if r == 0:
                    k = k + from_side(u_ref, j)
                if r == ROWS - 1:
                    k = k + from_side(d_ref, j)
                held[tile, 0, at, :] = k.astype(BF)
                held[tile, 1, at, :] = rows[r + 1][j].astype(BF)
                held[tile, 2, at, :] = conv[r][j].astype(BF)
        put(step).start()

    @pl.loop(0, chp // 16)
    def _(step):
        put(step).wait()


def per_device(query, key, value, control, kernel, grad_out, detail_blocks):
    shape = query.shape
    channels = shape[2]
    planes = lax.axis_size("z")
    cols = lax.axis_size("c")
    peers = ROWS * cols
    heads = HEADS // peers
    ch = heads * HEAD_DIM
    chp = -(-ch // 16) * 16
    plane = ("x", "c")
    my_z = lax.axis_index("z")
    my_col = lax.axis_index("c")
    me = lax.axis_index("x") * cols + my_col

    def flat(x):
        return x.reshape(LANES, channels)

    def swap(x):
        return lax.all_to_all(x.reshape(peers, -1, LANES), plane, 0, 0, tiled=True)

    def pack(arrays, *live):
        parts = len(arrays)
        rows = parts * chp + 16 * len(live)
        (out,) = call(
            functools.partial(pack_body, parts, ch, chp),
            [((peers, rows, LANES), BF)],
            *[flat(x) for x in arrays], *live,
            scratch=[
                pltpu.VMEM((parts, LANES, channels), BF),
                pltpu.VMEM((peers, rows, LANES), BF),
                pltpu.SemaphoreType.DMA((3, parts)),
            ],
            mib=56,
            far_in=range(parts),
            far_out=(0,),
        )
        return out

    sent = pack([key, value, control])
    mine = swap(sent).reshape(peers, 3, chp, LANES)
    wanted = lax.dynamic_index_in_dim(detail_blocks[0], my_col, 0, keepdims=False)
    named = (wanted >= 0) | (jnp.arange(cols) == my_col)
    named = jnp.concatenate([named, jnp.stack([my_z >= 1, my_z + 1 < planes])])
    live = jnp.where(jnp.pad(named, (0, 14 - cols)), 0.0, NEG).astype(F32)
    live = jnp.broadcast_to(live[:, None], (16, LANES))
    sent_q = pack([query, grad_out], live)
    mine, sent_q = lax.optimization_barrier((mine, sent_q))
    down_pairs = [(i, i + 1) for i in range(planes - 1)]
    up_pairs = [(i + 1, i) for i in range(planes - 1)]
    rim = (3 * cols + cols // 2, chp, LANES)
    to_up, to_down = call(rim_body, [(rim, BF)] * 2, mine)
    below = lax.ppermute(to_up, "z", up_pairs)
    above = lax.ppermute(to_down, "z", down_pairs)

    coefs = lax.dynamic_slice_in_dim(kernel.reshape(9, channels), me * ch, ch, 1)
    coefs = jnp.pad(coefs.T, ((0, chp - ch), (0, LANES - 9)))
    queries = swap(sent_q)

    wide = cols * LANES

    def tiles(*lead):
        return lead + (chp, LANES), BF

    mine, above, below = call(
        values_body,
        [(x.shape, BF) for x in (mine, above, below)],
        mine, above, below, coefs,
        flops=4 * 10**9,
        aliases={0: 0, 1: 1, 2: 2},
    )
    side = (2 * cols + cols // 2, chp, LANES)
    flops = 10 * peers * heads * LANES * (wide + 2 * LANES) * 256
    dq, to_up, to_down, dk, dv = call(
        functools.partial(attend_body, heads),
        [
            ((peers, chp, LANES), BF),
            (side, BF),
            (side, BF),
            ((ROWS, chp, wide), F32),
            ((ROWS, chp, wide), F32),
        ],
        queries, mine, above, below,
        flops=flops,
        mib=6,
    )
    from_above = lax.ppermute(to_down, "z", down_pairs)
    from_below = lax.ppermute(to_up, "z", up_pairs)

    own = ((ROWS, chp, wide), F32)
    sent_dq, dk, dv = call(
        functools.partial(kernel_grad_body, ch),
        [((peers, chp + 32, LANES), BF), own, own],
        dq, mine, above, below, dk, dv, to_up, to_down,
        scratch=[
            pltpu.VMEM((chp, LANES), F32),
            pltpu.VMEM((peers, 32, LANES), BF),
            pltpu.SemaphoreType.DMA((4,)),
        ],
        far_out=(0, 1, 2),
        hbm=(1, 2),
        flops=4 * 10**9,
    )
    dq_back = swap(sent_dq)

    (results,) = call(
        finish_body, [tiles(peers, 3)],
        *[pltpu.with_memory_space_constraint(x, pltpu.HBM) for x in (dk, dv)],
        to_up, to_down, from_below, from_above, coefs,
        scratch=[
            pltpu.VMEM((ROWS, chp, wide), F32),
            pltpu.VMEM((ROWS, chp, wide), F32),
            pltpu.VMEM((peers, 3, chp, LANES), BF),
            pltpu.SemaphoreType.DMA((3, chp // 16)),
        ],
        far_in=(0, 1),
        far_out=(0,),
        flops=4 * 10**9,
    )
    back = swap(results).reshape(peers, 3, chp, LANES)
    grad_query, taps_sum = call(
        functools.partial(unpack_query_body, ch, chp),
        [((LANES, channels), BF), ((16, channels), F32)],
        dq_back,
    )
    step = 1
    while 2 * step < planes:
        other = lax.ppermute(taps_sum, "z", [(i, i ^ step) for i in range(planes)])
        (taps_sum,) = call(add_body, [((16, channels), F32)], taps_sum, other)
        step *= 2
    other = lax.ppermute(taps_sum, "z", [(i, i ^ step) for i in range(planes)])
    (grad_kernel,) = call(taps_out_body, [((3, 3, channels), F32)], taps_sum, other)
    outs = call(functools.partial(unpack_body, ch), [((LANES, channels), BF)] * 3, back)
    return tuple(x.reshape(shape) for x in [grad_query] + list(outs)) + (grad_kernel,)


def solution(mesh):
    trow, tcol = mesh.shape["trow"], mesh.shape["tcol"]
    grid = Mesh(mesh.devices.reshape(trow // ROWS, ROWS, tcol), ("z", "x", "c"))
    tiled = P(("z", "x"), "c", None)
    return jax.shard_map(
        per_device,
        mesh=grid,
        in_specs=(tiled, tiled, tiled, tiled, P(), tiled, P(("z", "x"), None, None)),
        out_specs=(tiled, tiled, tiled, tiled, P()),
        check_vma=False,
    )
```

```python
import functools
import math

import jax
import jax.numpy as jnp
from jax import lax
from jax.experimental import pallas as pl
from jax.experimental.pallas import tpu as pltpu
from jax.sharding import Mesh, PartitionSpec as P

HEADS = 16
HEAD_DIM = 72
ROWS = 2
LANES = 128
HALF = 64
NEG = -1e30
INV_ROOT = HEAD_DIM ** (-0.5)
LOG2E = 1.4426950408889634
BF = jnp.bfloat16
F32 = jnp.float32


def params(mib):
    return pltpu.CompilerParams(vmem_limit_bytes=mib << 20)


ANY = pl.BlockSpec(memory_space=pl.ANY)
VMEM = pl.BlockSpec(memory_space=pltpu.VMEM)


def call(body, outs, *args, scratch=(), flops=0, mib=8, aliases=None, far_in=(), far_out=(), hbm=()):
    moved = sum(a.size * a.dtype.itemsize for a in args)
    moved += sum(math.prod(shape) * jnp.dtype(dtype).itemsize for shape, dtype in outs)
    return pl.pallas_call(
        body,
        out_shape=[
            (pltpu.HBM if n in hbm else jax.ShapeDtypeStruct)(shape, dtype)
            for n, (shape, dtype) in enumerate(outs)
        ],
        in_specs=[ANY if n in far_in else VMEM for n in range(len(args))],
        out_specs=[ANY if n in far_out else VMEM for n in range(len(outs))],
        scratch_shapes=list(scratch),
        input_output_aliases=aliases or {},
        compiler_params=params(mib),
        cost_estimate=pl.CostEstimate(flops=flops, bytes_accessed=moved, transcendentals=0),
    )(*args)


def facing(body, *places):
    def kernel(*refs):
        odd = lax.rem(lax.axis_index("z"), 2)
        turned = list(refs)
        for place in places:
            turned[place], turned[place + 1] = refs[place + 1], refs[place]

        @pl.when(odd == 1)
        def _():
            body(*refs)

        @pl.when(odd == 0)
        def _():
            body(*turned)

    return kernel


def my_halves():
    odd = lax.rem(lax.axis_index("c"), 2)
    return [pl.ds(pl.multiple_of(x * HALF, HALF), HALF) for x in (odd, 1 - odd)]


def store_halves(out, x):
    for i, half in enumerate(my_halves()):
        out[half] = x[i * HALF : (i + 1) * HALF]


def pack_body(parts, ch, chp, *refs):
    ins = refs[:parts]
    live, out = refs[parts:-4], refs[-4]
    held, packed, sems = refs[-3:]
    halves = my_halves()

    def get(n):
        return [
            pltpu.make_async_copy(
                ins[n].at[halves[i]], held.at[n, pl.ds(i * HALF, HALF)], sems.at[i, n]
            )
            for i in range(2)
        ]

    for n in range(parts):
        for copy in get(n):
            copy.start()
    backs = []
    for n in range(parts):
        for copy in get(n):
            copy.wait()
        x = held[n]
        if ch % 16:
            x = x.astype(F32)
        x = x.T
        rows = pl.ds(n * chp, chp)
        for p in range(out.shape[0]):
            piece = x[p * ch : (p + 1) * ch]
            if chp > ch:
                piece = jnp.concatenate([piece, jnp.zeros((chp - ch, LANES), piece.dtype)], axis=0)
            packed[p, n * chp : (n + 1) * chp] = piece.astype(BF)
        if n == parts - 1 and live:
            for p in range(out.shape[0]):
                packed[p, parts * chp :] = live[0][...].astype(BF)
            rows = pl.ds(n * chp, chp + 16)
        backs.append(pltpu.make_async_copy(packed.at[:, rows], out.at[:, rows], sems.at[2, n]))
        backs[n].start()
    for back in backs:
        back.wait()


def unpack_body(ch, x_ref, *outs):
    peers = x_ref.shape[0]
    for n, out in enumerate(outs):
        pieces = [x_ref[p, n] for p in range(peers)]
        if ch % 16:
            pieces = [piece.astype(F32)[:ch] for piece in pieces]
        store_halves(out, jnp.concatenate(pieces, axis=0).T.astype(BF))


def unpack_query_body(ch, chp, x_ref, out, gk_ref):
    peers = x_ref.shape[0]
    pieces = [x_ref[p, :chp] for p in range(peers)]
    if ch % 16:
        pieces = [piece.astype(F32)[:ch] for piece in pieces]
    store_halves(out, jnp.concatenate(pieces, axis=0).T.astype(BF))
    wide = gk_ref.shape[1]
    total = [jnp.zeros((16, LANES), F32) for _ in range(wide // LANES + 2)]
    lane = lax.broadcasted_iota(jnp.int32, (16, LANES), 1)
    for p in range(peers):
        table = x_ref[p, chp:].astype(F32)
        pieces = [table[:16] + pltpu.roll(table, 32 - 9, 0)[:16]]
        if ch > LANES:
            more = pltpu.roll(table, 32 - 18, 0)[:16]
            more = more + pltpu.roll(more, 2 * LANES - ch, 1)
            pieces.append(jnp.where(lane < ch - LANES, more, 0.0))
        first, off = divmod(p * ch, LANES)
        for b, piece in enumerate(pieces):
            turned = pltpu.roll(piece, off, 1) if off else piece
            total[first + b] = total[first + b] + jnp.where(lane >= off, turned, 0.0)
            if off:
                total[first + b + 1] = total[first + b + 1] + jnp.where(lane < off, turned, 0.0)
    gk_ref[...] = jnp.concatenate(total[: wide // LANES], axis=1)


def taps_out_body(x_ref, y_ref, out):
    total = x_ref[...] + y_ref[...]
    for a in range(3):
        out[a] = total[3 * a : 3 * a + 3]


def add_body(x_ref, y_ref, out):
    out[...] = x_ref[...] + y_ref[...]


def second_rows(rows):
    lane = lax.broadcasted_iota(jnp.int32, (rows, LANES), 1)
    return lane >= HALF, lane < HALF


def lane_masks(rows):
    col = lax.broadcasted_iota(jnp.int32, (rows, LANES), 1) & (HALF - 1)
    return second_rows(rows), col == 0, col == HALF - 1


def col_shifts(tiles, masks):
    _, first, last = masks
    none = jnp.zeros_like(tiles[0])
    out = []
    for j, t in enumerate(tiles):
        before = tiles[j - 1] if j else none
        after = tiles[j + 1] if j + 1 < len(tiles) else none
        out.append(
            (
                pltpu.roll(jnp.where(last, before, t), 1, 1),
                t,
                pltpu.roll(jnp.where(first, after, t), LANES - 1, 1),
            )
        )
    return out


def merge(tiles_second, tiles_first, masks):
    second = masks[0]
    return [
        jnp.where(second[j % 2], x, y) for j, (x, y) in enumerate(zip(tiles_second, tiles_first))
    ]


def row_terms(tiles, coef, masks):
    return [
        [sum(coef[3 * a + b] * t[b] for b in range(3)) for a in range(3)]
        for t in col_shifts(tiles, masks)
    ]


def edge_terms(tiles, coef, masks):
    second = masks[0]
    mixed = [[jnp.where(second[p], coef[b], coef[6 + b]) for b in range(3)] for p in range(2)]
    return [
        sum(mixed[j % 2][b] * t[b] for b in range(3))
        for j, t in enumerate(col_shifts(tiles, masks))
    ]


def turn(x):
    return pltpu.roll(x, HALF, 1)


def conv_pair(first, last, edge, coef, masks):
    second = masks[0]
    top, bottom = row_terms(first, coef, masks), row_terms(last, coef, masks)
    out = ([], [])
    for j, ((tu, tm, td), (bu, bm, bd)) in enumerate(zip(top, bottom)):
        e = edge[j] if edge else 0.0
        out[0].append(tm + turn(jnp.where(second[j % 2], e + td, tu + bd)))
        out[1].append(bm + turn(jnp.where(second[j % 2], tu + bd, bu + e)))
    return out


def taps(kc_ref, at):
    block = kc_ref[at, :]
    return [jnp.broadcast_to(block[:, t : t + 1], (16, LANES)) for t in range(9)]


def rim_body(a_ref, up_ref, down_ref):
    cols = a_ref.shape[0] // ROWS
    second = second_rows(a_ref.shape[2])
    for out, row, further, want in ((up_ref, 0, 1, 0), (down_ref, ROWS - 1, ROWS - 2, 1)):
        for j in range(cols):
            for n in range(3):
                out[n * cols + j] = a_ref[row * cols + j, n]
        for m in range(0, cols, 2):
            even, odd = (a_ref[further * cols + m + i, 2].astype(F32) for i in range(2))
            out[3 * cols + m // 2] = jnp.where(second[want], odd, even).astype(BF)


def outer_controls(u_ref, d_ref, at, masks):
    half = u_ref.shape[0] * 2 // 7
    above, below = (
        [ref[3 * half + j // 2, at, :].astype(F32) for j in range(half)] for ref in (u_ref, d_ref)
    )
    return merge(above, below, masks)


def load(ref, first, count, at):
    return [ref[first + j, at, :].astype(F32) for j in range(count)]


def load_own(a_ref, r, n, at):
    cols = a_ref.shape[0] // ROWS
    return [a_ref[r * cols + j, n, at, :].astype(F32) for j in range(cols)]


def own_values_body(a_ref, kc_ref, a_out, part_ref):
    cols = a_ref.shape[0] // ROWS

    @pl.loop(0, a_ref.shape[2] // 16)
    def _(step):
        at = pl.ds(pl.multiple_of(step * 16, 16), 16)
        masks = lane_masks(16)
        second = masks[0]
        conv = conv_pair(
            load_own(a_ref, 0, 2, at), load_own(a_ref, 1, 2, at), None, taps(kc_ref, at), masks
        )
        for j in range(cols):
            part_ref[j, at, :] = jnp.where(second[j % 2], conv[1][j], conv[0][j])
            for r in range(ROWS):
                tile = r * cols + j
                value = a_ref[tile, 1, at, :].astype(F32)
                inner = second[j % 2] if r == 0 else second[1 - j % 2]
                a_out[tile, 0, at, :] = a_ref[tile, 0, at, :]
                a_out[tile, 1, at, :] = jnp.where(inner, value + conv[r][j], value).astype(BF)
                a_out[tile, 2, at, :] = a_ref[tile, 2, at, :]


def values_body(a_ref, u_ref, d_ref, part_ref, kc_ref, a_out, u_out, d_out):
    cols = a_ref.shape[0] // ROWS

    @pl.loop(0, a_ref.shape[2] // 16)
    def _(step):
        at = pl.ds(pl.multiple_of(step * 16, 16), 16)
        masks = lane_masks(16)
        second = masks[0]
        coef = taps(kc_ref, at)
        far = edge_terms(outer_controls(u_ref, d_ref, at, masks), coef, masks)
        own = merge(load_own(a_ref, ROWS - 1, 2, at), load_own(a_ref, 0, 2, at), masks)
        own = edge_terms(own, coef, masks)
        above = row_terms(load(u_ref, 2 * cols, cols, at), coef, masks)
        below = row_terms(load(d_ref, 2 * cols, cols, at), coef, masks)
        for ref, out in ((u_ref, u_out), (d_ref, d_out)):
            for n in range(ref.shape[0]):
                if not cols <= n < 2 * cols:
                    out[n, at, :] = ref[n, at, :]
        for j in range(cols):
            (uu, um, ud), (du, dm, dd) = above[j], below[j]
            pick = second[j % 2]
            u_conv = um + turn(jnp.where(pick, far[j] + ud, uu + own[j]))
            d_conv = dm + turn(jnp.where(pick, own[j] + dd, du + far[j]))
            rim = part_ref[j, at, :] + turn(jnp.where(pick, uu, dd))
            u_out[cols + j, at, :] = (u_ref[cols + j, at, :].astype(F32) + u_conv).astype(BF)
            d_out[cols + j, at, :] = (d_ref[cols + j, at, :].astype(F32) + d_conv).astype(BF)
            for r in range(ROWS):
                tile = r * cols + j
                value = a_ref[tile, 1, at, :].astype(F32)
                inner = pick if r == 0 else second[1 - j % 2]
                a_out[tile, 0, at, :] = a_ref[tile, 0, at, :]
                a_out[tile, 1, at, :] = jnp.where(inner, value, value + rim).astype(BF)
                a_out[tile, 2, at, :] = a_ref[tile, 2, at, :]


def attend_body(heads, q_ref, a_ref, u_ref, d_ref, dq_ref, up_ref, down_ref, dk_ref, dv_ref):
    peers = q_ref.shape[0]
    cols = peers // ROWS
    chp = a_ref.shape[2]
    wide = cols * LANES

    dk_ref[...] = jnp.zeros_like(dk_ref)
    dv_ref[...] = jnp.zeros_like(dv_ref)
    chan = lax.broadcasted_iota(jnp.int32, (chp, LANES), 0)
    mine = [(chan >= h * HEAD_DIM) & (chan < (h + 1) * HEAD_DIM) for h in range(heads)]

    def spread(x):
        x = x.astype(F32)
        return jnp.concatenate([jnp.where(m, x, 0.0) for m in mine], axis=1).astype(BF)

    def dot(x, y, on_x, on_y):
        return lax.dot_general(
            x, y, (((on_x,), (on_y,)), ((), ())), preferred_element_type=F32
        )

    def front(tile):
        r, j = divmod(tile, cols)
        q = spread(q_ref[tile, :chp])
        g = spread(q_ref[tile, chp : 2 * chp])

        def all_keys(n):
            above = u_ref[n * cols + j] if r == 0 else a_ref[tile - cols, n]
            below = d_ref[n * cols + j] if r == ROWS - 1 else a_ref[tile + cols, n]
            row = [a_ref[r * cols + p, n] for p in range(cols)]
            return jnp.concatenate(row + [above, below], axis=1)

        k = all_keys(0)
        return q, g, k, dot(q, k, 0, 0), dot(g, all_keys(1), 0, 0)

    def middle(tile, s, gw):
        r = tile // cols
        live = q_ref[tile, 2 * chp :].astype(F32)
        zero = jnp.zeros((1, LANES), F32)
        bias = jnp.concatenate(
            [live[p : p + 1] for p in range(cols)]
            + [
                live[cols : cols + 1] if r == 0 else zero,
                live[cols + 1 : cols + 2] if r == ROWS - 1 else zero,
            ],
            axis=1,
        )
        s = s + bias
        top = jnp.max(s, axis=1, keepdims=True)
        e = jnp.exp2((s - top) * (INV_ROOT * LOG2E))
        w = e * (1.0 / jnp.sum(e, axis=1, keepdims=True))
        delta = jnp.sum(w * gw, axis=1, keepdims=True)
        return w.astype(BF), (w * (gw - delta)).astype(BF)

    def back(tile, q, g, k, w, gs):
        r, j = divmod(tile, cols)
        span = slice(j * LANES, (j + 1) * LANES)
        dk = dot(q, gs, 1, 0)
        dv = dot(g, w, 1, 0)
        dq = dot(k, gs, 1, 1)
        own = dq[:, :LANES]
        for h in range(1, heads):
            own = jnp.where(mine[h], dq[:, h * LANES : (h + 1) * LANES], own)
        dq_ref[tile] = (own * INV_ROOT).astype(BF)
        dk_ref[r] += dk[:, :wide]
        dv_ref[r] += dv[:, :wide]
        for side, at in ((r - 1, wide), (r + 1, wide + LANES)):
            dk_side, dv_side = dk[:, at : at + LANES], dv[:, at : at + LANES]
            if 0 <= side < ROWS:
                dk_ref[side, :, span] += dk_side
                dv_ref[side, :, span] += dv_side
            else:
                out = up_ref if side < 0 else down_ref
                out[j] = (dk_side * INV_ROOT).astype(BF)
                out[cols + j] = dv_side.astype(BF)

    ahead = front(0)
    for tile in range(peers):
        q, g, k, s, gw = ahead
        if tile + 1 < peers:
            ahead = front(tile + 1)
        halves = [middle(tile, s[i : i + 64], gw[i : i + 64]) for i in range(0, s.shape[0], 64)]
        w, gs = (jnp.concatenate(x, axis=0) for x in zip(*halves))
        back(tile, q, g, k, w, gs)

    second = second_rows(chp)
    for out, row, want in ((up_ref, 0, 0), (down_ref, ROWS - 1, 1)):
        for m in range(0, cols, 2):
            even, odd = (dv_ref[row, :, (m + i) * LANES : (m + i + 1) * LANES] for i in range(2))
            out[2 * cols + m // 2] = jnp.where(second[1 - want], even, odd).astype(BF)


def value_terms(dv_ref, up_ref, down_ref, i, j, at):
    cols = dv_ref.shape[2] // LANES
    if i == 0:
        return up_ref[cols + j, at, :].astype(F32)
    if i == ROWS + 1:
        return down_ref[cols + j, at, :].astype(F32)
    return dv_ref[i - 1, at, j * LANES : (j + 1) * LANES]


def kernel_grad_body(
    ch, dq_ref, a_ref, u_ref, d_ref, dk_ref, dv_ref, up_ref, down_ref, out_ref, dk_out, dv_out, sums, rows, sems
):
    cols = dv_ref.shape[2] // LANES
    chp = dv_ref.shape[1]
    copies = [
        pltpu.make_async_copy(dq_ref, out_ref.at[:, pl.ds(0, chp)], sems.at[0]),
        pltpu.make_async_copy(dk_ref, dk_out, sems.at[1]),
        pltpu.make_async_copy(dv_ref, dv_out, sems.at[2]),
    ]
    for copy in copies:
        copy.start()

    @pl.loop(0, chp // 16)
    def _(step):
        at = pl.ds(pl.multiple_of(step * 16, 16), 16)
        masks = lane_masks(16)
        second = masks[0]
        acc = [jnp.zeros((16, LANES), F32) for _ in range(9)]
        outer = col_shifts(outer_controls(u_ref, d_ref, at, masks), masks)
        above, here = outer, col_shifts(load(u_ref, 2 * cols, cols, at), masks)
        for i in range(ROWS + 2):
            if i < ROWS:
                below = col_shifts(load_own(a_ref, i, 2, at), masks)
            elif i == ROWS:
                below = col_shifts(load(d_ref, 2 * cols, cols, at), masks)
            else:
                below = outer
            for j in range(cols):
                g = value_terms(dv_ref, up_ref, down_ref, i, j, at)
                turned = turn(g)
                for b in range(3):
                    acc[b] += jnp.where(second[j % 2], above[j][b], here[j][b]) * turned
                    acc[3 + b] += here[j][b] * g
                    acc[6 + b] += jnp.where(second[j % 2], here[j][b], below[j][b]) * turned
            above, here = here, below
        lane = lax.broadcasted_iota(jnp.int32, (16, LANES), 1)
        out = jnp.zeros((16, LANES), F32)
        for t in range(9):
            out = jnp.where(lane == t, jnp.sum(acc[t], axis=1, keepdims=True), out)
        sums[at, :] = out

    def split(x):
        high = x.astype(BF).astype(F32)
        return high, x - high

    high, low = split(sums[: min(chp, LANES)])
    table = high + pltpu.roll(low, 9, 1)
    if chp < LANES:
        table = jnp.concatenate([table, jnp.zeros((LANES - chp, LANES), F32)], axis=0)
    if chp > LANES:
        more = jnp.concatenate(split(sums[LANES:]), axis=0)
        more = jnp.concatenate([more, jnp.zeros((LANES - more.shape[0], LANES), F32)], axis=0)
        table = table + pltpu.roll(more, 18, 1)
    table = table.T[:32].astype(BF)
    for tile in range(rows.shape[0]):
        rows[tile] = table
    sums_out = pltpu.make_async_copy(rows, out_ref.at[:, pl.ds(chp, 32)], sems.at[3])
    sums_out.start()
    for copy in copies + [sums_out]:
        copy.wait()


def finish_body(
    dk_hbm, dv_hbm, up_ref, down_ref, u_ref, d_ref, kc_ref, out_ref, dk_ref, dv_ref, held, sems
):
    cols = held.shape[0] // ROWS
    chp = held.shape[2]

    def chunk(step):
        return pl.ds(pl.multiple_of(step * 16, 16), 16)

    def get(step):
        at = chunk(step)
        return [
            pltpu.make_async_copy(dk_hbm.at[:, at], dk_ref.at[:, at], sems.at[0, step]),
            pltpu.make_async_copy(dv_hbm.at[:, at], dv_ref.at[:, at], sems.at[1, step]),
        ]

    def put(step):
        at = chunk(step)
        return pltpu.make_async_copy(held.at[:, :, at], out_ref.at[:, :, at], sems.at[2, step])

    @pl.loop(0, chp // 16)
    def _(step):
        for copy in get(step):
            copy.start()

    @pl.loop(0, chp // 16)
    def _(step):
        for copy in get(step):
            copy.wait()
        at = chunk(step)
        masks = lane_masks(16)
        coef = taps(kc_ref, at)[::-1]

        def from_side(ref, n):
            return ref[n, at, :].astype(F32)

        def rounded(x):
            return x.astype(BF).astype(F32)

        rows = []
        for i in range(ROWS + 2):
            row = []
            for j in range(cols):
                x = value_terms(dv_ref, up_ref, down_ref, i, j, at)
                if i == 0:
                    rim = from_side(u_ref, 2 * cols + j // 2)
                    x = x + rim
                elif i == ROWS + 1:
                    rim = from_side(d_ref, 2 * cols + j // 2)
                    x = x + rim
                else:
                    if i == 1:
                        x = x + from_side(u_ref, cols + j)
                    if i == ROWS:
                        x = x + from_side(d_ref, cols + j)
                row.append(rounded(x))
            rows.append(row)
        edge = edge_terms(merge(rows[0], rows[-1], masks), coef, masks)
        conv = conv_pair(rows[1], rows[2], edge, coef, masks)
        for r in range(ROWS):
            for j in range(cols):
                tile = r * cols + j
                k = dk_ref[r, at, j * LANES : (j + 1) * LANES] * INV_ROOT
                if r == 0:
                    k = k + from_side(u_ref, j)
                if r == ROWS - 1:
                    k = k + from_side(d_ref, j)
                held[tile, 0, at, :] = k.astype(BF)
                held[tile, 1, at, :] = rows[r + 1][j].astype(BF)
                held[tile, 2, at, :] = conv[r][j].astype(BF)
        put(step).start()

    @pl.loop(0, chp // 16)
    def _(step):
        put(step).wait()


def per_device(query, key, value, control, kernel, grad_out, detail_blocks):
    shape = query.shape
    channels = shape[2]
    planes = lax.axis_size("z")
    cols = lax.axis_size("c")
    peers = ROWS * cols
    heads = HEADS // peers
    ch = heads * HEAD_DIM
    chp = -(-ch // 16) * 16
    plane = ("x", "c")
    my_z = lax.axis_index("z")
    my_col = lax.axis_index("c")
    me = lax.axis_index("x") * cols + my_col

    def flat(x):
        return x.reshape(LANES, channels)

    def swap(x):
        return lax.all_to_all(x.reshape(peers, -1, LANES), plane, 0, 0, tiled=True)

    def pack(arrays, *live):
        parts = len(arrays)
        rows = parts * chp + 16 * len(live)
        (out,) = call(
            functools.partial(pack_body, parts, ch, chp),
            [((peers, rows, LANES), BF)],
            *[flat(x) for x in arrays], *live,
            scratch=[
                pltpu.VMEM((parts, LANES, channels), BF),
                pltpu.VMEM((peers, rows, LANES), BF),
                pltpu.SemaphoreType.DMA((3, parts)),
            ],
            mib=56,
            far_in=range(parts),
            far_out=(0,),
        )
        return out

    sent = pack([key, value, control])
    mine = swap(sent).reshape(peers, 3, chp, LANES)
    wanted = lax.dynamic_index_in_dim(detail_blocks[0], my_col, 0, keepdims=False)
    named = (wanted >= 0) | (jnp.arange(cols) == my_col)
    named = jnp.concatenate([named, jnp.stack([my_z >= 1, my_z + 1 < planes])])
    live = jnp.where(jnp.pad(named, (0, 14 - cols)), 0.0, NEG).astype(F32)
    live = jnp.broadcast_to(live[:, None], (16, LANES))
    sent_q = pack([query, grad_out], live)
    mine, sent_q = lax.optimization_barrier((mine, sent_q))
    rounds = [
        [pair for i in range(start, planes - 1, 2) for pair in ((i, i + 1), (i + 1, i))]
        for start in range(2)
    ]

    def exchange(messages):
        return [lax.ppermute(x, "z", pairs) for x, pairs in zip(messages, rounds)]

    rim = (3 * cols + cols // 2, chp, LANES)
    sides = exchange(call(facing(rim_body, 1), [(rim, BF)] * 2, mine))

    coefs = lax.dynamic_slice_in_dim(kernel.reshape(9, channels), me * ch, ch, 1)
    coefs = jnp.pad(coefs.T, ((0, chp - ch), (0, LANES - 9)))
    queries = swap(sent_q)

    wide = cols * LANES

    def tiles(*lead):
        return lead + (chp, LANES), BF

    mine, part = call(
        own_values_body,
        [(mine.shape, BF), ((cols, chp, LANES), F32)],
        mine, coefs,
        flops=3 * 10**9,
        aliases={0: 0},
    )
    mine, *sides = call(
        facing(values_body, 1, 6),
        [(x.shape, BF) for x in (mine, *sides)],
        mine, *sides, part, coefs,
        flops=4 * 10**9,
        aliases={0: 0, 1: 1, 2: 2},
    )
    side = (2 * cols + cols // 2, chp, LANES)
    flops = 10 * peers * heads * LANES * (wide + 2 * LANES) * 256
    dq, *terms, dk, dv = call(
        facing(functools.partial(attend_body, heads), 2, 5),
        [
            ((peers, chp, LANES), BF),
            (side, BF),
            (side, BF),
            ((ROWS, chp, wide), F32),
            ((ROWS, chp, wide), F32),
        ],
        queries, mine, *sides,
        flops=flops,
        mib=6,
    )
    got_terms = exchange(terms)

    own = ((ROWS, chp, wide), F32)
    sent_dq, dk, dv = call(
        facing(functools.partial(kernel_grad_body, ch), 2, 6),
        [((peers, chp + 32, LANES), BF), own, own],
        dq, mine, *sides, dk, dv, *terms,
        scratch=[
            pltpu.VMEM((chp, LANES), F32),
            pltpu.VMEM((peers, 32, LANES), BF),
            pltpu.SemaphoreType.DMA((4,)),
        ],
        far_out=(0, 1, 2),
        hbm=(1, 2),
        flops=4 * 10**9,
    )
    dq_back = swap(sent_dq)

    (results,) = call(
        facing(finish_body, 2, 4), [tiles(peers, 3)],
        *[pltpu.with_memory_space_constraint(x, pltpu.HBM) for x in (dk, dv)],
        *terms, *got_terms, coefs,
        scratch=[
            pltpu.VMEM((ROWS, chp, wide), F32),
            pltpu.VMEM((ROWS, chp, wide), F32),
            pltpu.VMEM((peers, 3, chp, LANES), BF),
            pltpu.SemaphoreType.DMA((3, chp // 16)),
        ],
        far_in=(0, 1),
        far_out=(0,),
        flops=4 * 10**9,
    )
    back = swap(results).reshape(peers, 3, chp, LANES)
    grad_query, taps_sum = call(
        functools.partial(unpack_query_body, ch, chp),
        [((LANES, channels), BF), ((16, channels), F32)],
        dq_back,
    )
    step = 1
    while 2 * step < planes:
        other = lax.ppermute(taps_sum, "z", [(i, i ^ step) for i in range(planes)])
        (taps_sum,) = call(add_body, [((16, channels), F32)], taps_sum, other)
        step *= 2
    other = lax.ppermute(taps_sum, "z", [(i, i ^ step) for i in range(planes)])
    (grad_kernel,) = call(taps_out_body, [((3, 3, channels), F32)], taps_sum, other)
    outs = call(functools.partial(unpack_body, ch), [((LANES, channels), BF)] * 3, back)
    return tuple(x.reshape(shape) for x in [grad_query] + list(outs)) + (grad_kernel,)


def solution(mesh):
    trow, tcol = mesh.shape["trow"], mesh.shape["tcol"]
    grid = Mesh(mesh.devices.reshape(trow // ROWS, ROWS, tcol), ("z", "x", "c"))
    tiled = P(("z", "x"), "c", None)
    return jax.shard_map(
        per_device,
        mesh=grid,
        in_specs=(tiled, tiled, tiled, tiled, P(), tiled, P(("z", "x"), None, None)),
        out_specs=(tiled, tiled, tiled, tiled, P()),
        check_vma=False,
    )
```

```python
import functools
import math

import jax
import jax.numpy as jnp
from jax import lax
from jax.experimental import pallas as pl
from jax.experimental.pallas import tpu as pltpu
from jax.sharding import Mesh, PartitionSpec as P

HEADS = 16
HEAD_DIM = 72
ROWS = 2
LANES = 128
HALF = 64
NEG = -1e30
INV_ROOT = HEAD_DIM ** (-0.5)
LOG2E = 1.4426950408889634
BF = jnp.bfloat16
F32 = jnp.float32


def params(mib):
    return pltpu.CompilerParams(vmem_limit_bytes=mib << 20)


ANY = pl.BlockSpec(memory_space=pl.ANY)
VMEM = pl.BlockSpec(memory_space=pltpu.VMEM)


def call(body, outs, *args, scratch=(), flops=0, mib=8, aliases=None, far_in=(), far_out=(), hbm=()):
    moved = sum(a.size * a.dtype.itemsize for a in args)
    moved += sum(math.prod(shape) * jnp.dtype(dtype).itemsize for shape, dtype in outs)
    return pl.pallas_call(
        body,
        out_shape=[
            (pltpu.HBM if n in hbm else jax.ShapeDtypeStruct)(shape, dtype)
            for n, (shape, dtype) in enumerate(outs)
        ],
        in_specs=[ANY if n in far_in else VMEM for n in range(len(args))],
        out_specs=[ANY if n in far_out else VMEM for n in range(len(outs))],
        scratch_shapes=list(scratch),
        input_output_aliases=aliases or {},
        compiler_params=params(mib),
        cost_estimate=pl.CostEstimate(flops=flops, bytes_accessed=moved, transcendentals=0),
    )(*args)


def facing(body, *places):
    def kernel(*refs):
        odd = lax.rem(lax.axis_index("z"), 2)
        turned = list(refs)
        for place in places:
            turned[place], turned[place + 1] = refs[place + 1], refs[place]

        @pl.when(odd == 1)
        def _():
            body(*refs)

        @pl.when(odd == 0)
        def _():
            body(*turned)

    return kernel


def my_halves():
    odd = lax.rem(lax.axis_index("c"), 2)
    return [pl.ds(pl.multiple_of(x * HALF, HALF), HALF) for x in (odd, 1 - odd)]


def store_halves(out, x):
    for i, half in enumerate(my_halves()):
        out[half] = x[i * HALF : (i + 1) * HALF]


def pack_body(parts, ch, chp, *refs):
    ins = refs[:parts]
    live, out = refs[parts:-4], refs[-4]
    held, packed, sems = refs[-3:]
    halves = my_halves()

    def get(n):
        return [
            pltpu.make_async_copy(
                ins[n].at[halves[i]], held.at[n, pl.ds(i * HALF, HALF)], sems.at[i, n]
            )
            for i in range(2)
        ]

    for n in range(parts):
        for copy in get(n):
            copy.start()
    backs = []
    for n in range(parts):
        for copy in get(n):
            copy.wait()
        x = held[n]
        if ch % 16:
            x = x.astype(F32)
        x = x.T
        rows = pl.ds(n * chp, chp)
        for p in range(out.shape[0]):
            piece = x[p * ch : (p + 1) * ch]
            if chp > ch:
                piece = jnp.concatenate([piece, jnp.zeros((chp - ch, LANES), piece.dtype)], axis=0)
            packed[p, n * chp : (n + 1) * chp] = piece.astype(BF)
        if n == parts - 1 and live:
            for p in range(out.shape[0]):
                packed[p, parts * chp :] = live[0][...].astype(BF)
            rows = pl.ds(n * chp, chp + 16)
        backs.append(pltpu.make_async_copy(packed.at[:, rows], out.at[:, rows], sems.at[2, n]))
        backs[n].start()
    for back in backs:
        back.wait()


def unpack_body(ch, x_ref, *outs):
    peers = x_ref.shape[0]
    for n, out in enumerate(outs):
        pieces = [x_ref[p, n] for p in range(peers)]
        if ch % 16:
            pieces = [piece.astype(F32)[:ch] for piece in pieces]
        store_halves(out, jnp.concatenate(pieces, axis=0).T.astype(BF))


def unpack_query_body(ch, chp, x_ref, out, gk_ref):
    peers = x_ref.shape[0]
    pieces = [x_ref[p, :chp] for p in range(peers)]
    if ch % 16:
        pieces = [piece.astype(F32)[:ch] for piece in pieces]
    store_halves(out, jnp.concatenate(pieces, axis=0).T.astype(BF))
    count = out.shape[1] // LANES
    total = [jnp.zeros((16, LANES), F32) for _ in range(count + 2)]
    lane = lax.broadcasted_iota(jnp.int32, (16, LANES), 1)
    for p in range(peers):
        table = x_ref[p, chp:].astype(F32)
        pieces = [table[:16] + pltpu.roll(table, 32 - 9, 0)[:16]]
        if ch > LANES:
            more = pltpu.roll(table, 32 - 18, 0)[:16]
            more = more + pltpu.roll(more, 2 * LANES - ch, 1)
            pieces.append(jnp.where(lane < ch - LANES, more, 0.0))
        first, off = divmod(p * ch, LANES)
        for b, piece in enumerate(pieces):
            turned = pltpu.roll(piece, off, 1) if off else piece
            total[first + b] = total[first + b] + jnp.where(lane >= off, turned, 0.0)
            if off:
                total[first + b + 1] = total[first + b + 1] + jnp.where(lane < off, turned, 0.0)
    gk_ref[...] = jnp.zeros_like(gk_ref)
    for n in range(count):
        gk_ref[9 * n : 9 * n + 9] = total[n][:9]


def taps_out_body(x_ref, y_ref, out):
    total = x_ref[...] + y_ref[...]
    count = out.shape[2] // LANES
    total = jnp.concatenate([total[9 * n : 9 * n + 9] for n in range(count)], axis=1)
    for a in range(3):
        out[a] = total[3 * a : 3 * a + 3]


def add_body(x_ref, y_ref, out):
    out[...] = x_ref[...] + y_ref[...]


def chunks(rows):
    count = rows // 16
    return pl.loop(0, count, unroll=1 if count % 3 else 3)


def second_rows(rows):
    lane = lax.broadcasted_iota(jnp.int32, (rows, LANES), 1)
    return lane >= HALF, lane < HALF


def lane_masks(rows):
    col = lax.broadcasted_iota(jnp.int32, (rows, LANES), 1) & (HALF - 1)
    return second_rows(rows), col == 0, col == HALF - 1


def col_shifts(tiles, masks):
    _, first, last = masks
    none = jnp.zeros_like(tiles[0])
    out = []
    for j, t in enumerate(tiles):
        before = tiles[j - 1] if j else none
        after = tiles[j + 1] if j + 1 < len(tiles) else none
        out.append(
            (
                pltpu.roll(jnp.where(last, before, t), 1, 1),
                t,
                pltpu.roll(jnp.where(first, after, t), LANES - 1, 1),
            )
        )
    return out


def merge(tiles_second, tiles_first, masks):
    second = masks[0]
    return [
        jnp.where(second[j % 2], x, y) for j, (x, y) in enumerate(zip(tiles_second, tiles_first))
    ]


def row_terms(tiles, coef, masks):
    return [
        [sum(coef[3 * a + b] * t[b] for b in range(3)) for a in range(3)]
        for t in col_shifts(tiles, masks)
    ]


def edge_terms(tiles, coef, masks):
    second = masks[0]
    mixed = [[jnp.where(second[p], coef[b], coef[6 + b]) for b in range(3)] for p in range(2)]
    return [
        sum(mixed[j % 2][b] * t[b] for b in range(3))
        for j, t in enumerate(col_shifts(tiles, masks))
    ]


def turn(x):
    return pltpu.roll(x, HALF, 1)


def conv_pair(first, last, edge, coef, masks):
    second = masks[0]
    top, bottom = row_terms(first, coef, masks), row_terms(last, coef, masks)
    out = ([], [])
    for j, ((tu, tm, td), (bu, bm, bd)) in enumerate(zip(top, bottom)):
        e = edge[j] if edge else 0.0
        out[0].append(tm + turn(jnp.where(second[j % 2], e + td, tu + bd)))
        out[1].append(bm + turn(jnp.where(second[j % 2], tu + bd, bu + e)))
    return out


def taps(kc_ref, at):
    block = kc_ref[at, :]
    return [jnp.broadcast_to(block[:, t : t + 1], (16, LANES)) for t in range(9)]


def rim_body(a_ref, up_ref, down_ref):
    cols = a_ref.shape[0] // ROWS
    second = second_rows(a_ref.shape[2])
    for out, row, further, want in ((up_ref, 0, 1, 0), (down_ref, ROWS - 1, ROWS - 2, 1)):
        for j in range(cols):
            for n in range(3):
                out[n * cols + j] = a_ref[row * cols + j, n]
        for m in range(0, cols, 2):
            even, odd = (a_ref[further * cols + m + i, 2].astype(F32) for i in range(2))
            out[3 * cols + m // 2] = jnp.where(second[want], odd, even).astype(BF)


def outer_controls(u_ref, d_ref, at, masks):
    half = u_ref.shape[0] * 2 // 7
    above, below = (
        [ref[3 * half + j // 2, at, :].astype(F32) for j in range(half)] for ref in (u_ref, d_ref)
    )
    return merge(above, below, masks)


def load(ref, first, count, at):
    return [ref[first + j, at, :].astype(F32) for j in range(count)]


def load_own(a_ref, r, n, at):
    cols = a_ref.shape[0] // ROWS
    return [a_ref[r * cols + j, n, at, :].astype(F32) for j in range(cols)]


def own_values_body(a_ref, kc_ref, a_out, part_ref):
    cols = a_ref.shape[0] // ROWS

    @chunks(a_ref.shape[2])
    def _(step):
        at = pl.ds(pl.multiple_of(step * 16, 16), 16)
        masks = lane_masks(16)
        second = masks[0]
        conv = conv_pair(
            load_own(a_ref, 0, 2, at), load_own(a_ref, 1, 2, at), None, taps(kc_ref, at), masks
        )
        for j in range(cols):
            part_ref[j, at, :] = jnp.where(second[j % 2], conv[1][j], conv[0][j])
            for r in range(ROWS):
                tile = r * cols + j
                value = a_ref[tile, 1, at, :].astype(F32)
                inner = second[j % 2] if r == 0 else second[1 - j % 2]
                a_out[tile, 0, at, :] = a_ref[tile, 0, at, :]
                a_out[tile, 1, at, :] = jnp.where(inner, value + conv[r][j], value).astype(BF)
                a_out[tile, 2, at, :] = a_ref[tile, 2, at, :]


def values_body(a_ref, u_ref, d_ref, part_ref, kc_ref, a_out, u_out, d_out):
    cols = a_ref.shape[0] // ROWS

    @chunks(a_ref.shape[2])
    def _(step):
        at = pl.ds(pl.multiple_of(step * 16, 16), 16)
        masks = lane_masks(16)
        second = masks[0]
        coef = taps(kc_ref, at)
        far = edge_terms(outer_controls(u_ref, d_ref, at, masks), coef, masks)
        own = merge(load_own(a_ref, ROWS - 1, 2, at), load_own(a_ref, 0, 2, at), masks)
        own = edge_terms(own, coef, masks)
        above = row_terms(load(u_ref, 2 * cols, cols, at), coef, masks)
        below = row_terms(load(d_ref, 2 * cols, cols, at), coef, masks)
        for ref, out in ((u_ref, u_out), (d_ref, d_out)):
            for n in range(ref.shape[0]):
                if not cols <= n < 2 * cols:
                    out[n, at, :] = ref[n, at, :]
        for j in range(cols):
            (uu, um, ud), (du, dm, dd) = above[j], below[j]
            pick = second[j % 2]
            u_conv = um + turn(jnp.where(pick, far[j] + ud, uu + own[j]))
            d_conv = dm + turn(jnp.where(pick, own[j] + dd, du + far[j]))
            rim = part_ref[j, at, :] + turn(jnp.where(pick, uu, dd))
            u_out[cols + j, at, :] = (u_ref[cols + j, at, :].astype(F32) + u_conv).astype(BF)
            d_out[cols + j, at, :] = (d_ref[cols + j, at, :].astype(F32) + d_conv).astype(BF)
            for r in range(ROWS):
                tile = r * cols + j
                value = a_ref[tile, 1, at, :].astype(F32)
                inner = pick if r == 0 else second[1 - j % 2]
                a_out[tile, 0, at, :] = a_ref[tile, 0, at, :]
                a_out[tile, 1, at, :] = jnp.where(inner, value, value + rim).astype(BF)
                a_out[tile, 2, at, :] = a_ref[tile, 2, at, :]


def attend_body(heads, q_ref, a_ref, u_ref, d_ref, dq_ref, up_ref, down_ref, dk_ref, dv_ref):
    peers = q_ref.shape[0]
    cols = peers // ROWS
    chp = a_ref.shape[2]
    wide = cols * LANES

    dk_ref[...] = jnp.zeros_like(dk_ref)
    dv_ref[...] = jnp.zeros_like(dv_ref)
    chan = lax.broadcasted_iota(jnp.int32, (chp, LANES), 0)
    mine = [(chan >= h * HEAD_DIM) & (chan < (h + 1) * HEAD_DIM) for h in range(heads)]

    def spread(x):
        x = x.astype(F32)
        return jnp.concatenate([jnp.where(m, x, 0.0) for m in mine], axis=1).astype(BF)

    def dot(x, y, on_x, on_y):
        return lax.dot_general(
            x, y, (((on_x,), (on_y,)), ((), ())), preferred_element_type=F32
        )

    def front(tile):
        r, j = divmod(tile, cols)
        q = spread(q_ref[tile, :chp])
        g = spread(q_ref[tile, chp : 2 * chp])

        def all_keys(n):
            above = u_ref[n * cols + j] if r == 0 else a_ref[tile - cols, n]
            below = d_ref[n * cols + j] if r == ROWS - 1 else a_ref[tile + cols, n]
            row = [a_ref[r * cols + p, n] for p in range(cols)]
            return jnp.concatenate(row + [above, below], axis=1)

        k = all_keys(0)
        return q, g, k, dot(q, k, 0, 0), dot(g, all_keys(1), 0, 0)

    def middle(tile, s, gw):
        r = tile // cols
        live = q_ref[tile, 2 * chp :].astype(F32)
        zero = jnp.zeros((1, LANES), F32)
        bias = jnp.concatenate(
            [live[p : p + 1] for p in range(cols)]
            + [
                live[cols : cols + 1] if r == 0 else zero,
                live[cols + 1 : cols + 2] if r == ROWS - 1 else zero,
            ],
            axis=1,
        )
        s = s + bias
        top = jnp.max(s, axis=1, keepdims=True)
        e = jnp.exp2((s - top) * (INV_ROOT * LOG2E))
        w = e * (1.0 / jnp.sum(e, axis=1, keepdims=True))
        delta = jnp.sum(w * gw, axis=1, keepdims=True)
        return w.astype(BF), (w * (gw - delta)).astype(BF)

    def back(tile, q, g, k, w, gs):
        r, j = divmod(tile, cols)
        span = slice(j * LANES, (j + 1) * LANES)
        dk = dot(q, gs, 1, 0)
        dv = dot(g, w, 1, 0)
        dq = dot(k, gs, 1, 1)
        own = dq[:, :LANES]
        for h in range(1, heads):
            own = jnp.where(mine[h], dq[:, h * LANES : (h + 1) * LANES], own)
        dq_ref[tile] = (own * INV_ROOT).astype(BF)
        dk_ref[r] += dk[:, :wide]
        dv_ref[r] += dv[:, :wide]
        for side, at in ((r - 1, wide), (r + 1, wide + LANES)):
            dk_side, dv_side = dk[:, at : at + LANES], dv[:, at : at + LANES]
            if 0 <= side < ROWS:
                dk_ref[side, :, span] += dk_side
                dv_ref[side, :, span] += dv_side
            else:
                out = up_ref if side < 0 else down_ref
                out[j] = (dk_side * INV_ROOT).astype(BF)
                out[cols + j] = dv_side.astype(BF)

    ahead = front(0)
    for tile in range(peers):
        q, g, k, s, gw = ahead
        if tile + 1 < peers:
            ahead = front(tile + 1)
        halves = [middle(tile, s[i : i + 64], gw[i : i + 64]) for i in range(0, s.shape[0], 64)]
        w, gs = (jnp.concatenate(x, axis=0) for x in zip(*halves))
        back(tile, q, g, k, w, gs)

    second = second_rows(chp)
    for out, row, want in ((up_ref, 0, 0), (down_ref, ROWS - 1, 1)):
        for m in range(0, cols, 2):
            even, odd = (dv_ref[row, :, (m + i) * LANES : (m + i + 1) * LANES] for i in range(2))
            out[2 * cols + m // 2] = jnp.where(second[1 - want], even, odd).astype(BF)


def value_terms(dv_ref, up_ref, down_ref, i, j, at):
    cols = dv_ref.shape[2] // LANES
    if i == 0:
        return up_ref[cols + j, at, :].astype(F32)
    if i == ROWS + 1:
        return down_ref[cols + j, at, :].astype(F32)
    return dv_ref[i - 1, at, j * LANES : (j + 1) * LANES]


def kernel_grad_body(
    ch, dq_ref, a_ref, u_ref, d_ref, dk_ref, dv_ref, up_ref, down_ref, out_ref, dk_out, dv_out, sums, rows, sems
):
    cols = dv_ref.shape[2] // LANES
    chp = dv_ref.shape[1]
    copies = [
        pltpu.make_async_copy(dq_ref, out_ref.at[:, pl.ds(0, chp)], sems.at[0]),
        pltpu.make_async_copy(dk_ref, dk_out, sems.at[1]),
        pltpu.make_async_copy(dv_ref, dv_out, sems.at[2]),
    ]
    for copy in copies:
        copy.start()

    @chunks(chp)
    def _(step):
        at = pl.ds(pl.multiple_of(step * 16, 16), 16)
        masks = lane_masks(16)
        second = masks[0]
        acc = [jnp.zeros((16, LANES), F32) for _ in range(9)]
        outer = col_shifts(outer_controls(u_ref, d_ref, at, masks), masks)
        above, here = outer, col_shifts(load(u_ref, 2 * cols, cols, at), masks)
        for i in range(ROWS + 2):
            if i < ROWS:
                below = col_shifts(load_own(a_ref, i, 2, at), masks)
            elif i == ROWS:
                below = col_shifts(load(d_ref, 2 * cols, cols, at), masks)
            else:
                below = outer
            for j in range(cols):
                g = value_terms(dv_ref, up_ref, down_ref, i, j, at)
                turned = turn(g)
                for b in range(3):
                    acc[b] += jnp.where(second[j % 2], above[j][b], here[j][b]) * turned
                    acc[3 + b] += here[j][b] * g
                    acc[6 + b] += jnp.where(second[j % 2], here[j][b], below[j][b]) * turned
            above, here = here, below
        for n in range(9):
            sums[n, at, :] = acc[n]

    lane = lax.broadcasted_iota(jnp.int32, (chp, LANES), 1)
    whole = jnp.zeros((chp, LANES), F32)
    for t in range(9):
        whole = jnp.where(lane == t, jnp.sum(sums[t], axis=1, keepdims=True), whole)
    def split(x):
        high = x.astype(BF).astype(F32)
        return high, x - high

    high, low = split(whole[: min(chp, LANES)])
    table = high + pltpu.roll(low, 9, 1)
    if chp < LANES:
        table = jnp.concatenate([table, jnp.zeros((LANES - chp, LANES), F32)], axis=0)
    if chp > LANES:
        more = jnp.concatenate(split(whole[LANES:]), axis=0)
        more = jnp.concatenate([more, jnp.zeros((LANES - more.shape[0], LANES), F32)], axis=0)
        table = table + pltpu.roll(more, 18, 1)
    table = table.T[:32].astype(BF)
    for tile in range(rows.shape[0]):
        rows[tile] = table
    sums_out = pltpu.make_async_copy(rows, out_ref.at[:, pl.ds(chp, 32)], sems.at[3])
    sums_out.start()
    for copy in copies + [sums_out]:
        copy.wait()


def finish_body(
    dk_hbm, dv_hbm, up_ref, down_ref, u_hbm, d_hbm, kc_ref, out_ref, dk_ref, dv_ref, u_ref, d_ref, held, sems, ends
):
    cols = held.shape[0] // ROWS
    chp = held.shape[2]

    def chunk(step):
        return pl.ds(pl.multiple_of(step * 16, 16), 16)

    def put(step):
        at = chunk(step)
        return pltpu.make_async_copy(held.at[:, :, at], out_ref.at[:, :, at], ends.at[step])

    gets = [
        pltpu.make_async_copy(*pair, sems.at[n])
        for n, pair in enumerate(
            ((u_hbm, u_ref), (d_hbm, d_ref), (dk_hbm, dk_ref), (dv_hbm, dv_ref))
        )
    ]
    for get in gets:
        get.start()
    for get in gets:
        get.wait()

    @pl.loop(0, chp // 16)
    def _(step):
        at = chunk(step)
        masks = lane_masks(16)
        coef = taps(kc_ref, at)[::-1]

        def from_side(ref, n):
            return ref[n, at, :].astype(F32)

        def rounded(x):
            return x.astype(BF).astype(F32)

        rows = []
        for i in range(ROWS + 2):
            row = []
            for j in range(cols):
                x = value_terms(dv_ref, up_ref, down_ref, i, j, at)
                if i == 0:
                    rim = from_side(u_ref, 2 * cols + j // 2)
                    x = x + rim
                elif i == ROWS + 1:
                    rim = from_side(d_ref, 2 * cols + j // 2)
                    x = x + rim
                else:
                    if i == 1:
                        x = x + from_side(u_ref, cols + j)
                    if i == ROWS:
                        x = x + from_side(d_ref, cols + j)
                row.append(rounded(x))
            rows.append(row)
        edge = edge_terms(merge(rows[0], rows[-1], masks), coef, masks)
        conv = conv_pair(rows[1], rows[2], edge, coef, masks)
        for r in range(ROWS):
            for j in range(cols):
                tile = r * cols + j
                k = dk_ref[r, at, j * LANES : (j + 1) * LANES] * INV_ROOT
                if r == 0:
                    k = k + from_side(u_ref, j)
                if r == ROWS - 1:
                    k = k + from_side(d_ref, j)
                held[tile, 0, at, :] = k.astype(BF)
                held[tile, 1, at, :] = rows[r + 1][j].astype(BF)
                held[tile, 2, at, :] = conv[r][j].astype(BF)
        put(step).start()

    @pl.loop(0, chp // 16)
    def _(step):
        put(step).wait()


def per_device(query, key, value, control, kernel, grad_out, detail_blocks):
    shape = query.shape
    channels = shape[2]
    planes = lax.axis_size("z")
    cols = lax.axis_size("c")
    peers = ROWS * cols
    heads = HEADS // peers
    ch = heads * HEAD_DIM
    chp = -(-ch // 16) * 16
    plane = ("x", "c")
    my_z = lax.axis_index("z")
    my_col = lax.axis_index("c")
    me = lax.axis_index("x") * cols + my_col

    def flat(x):
        return x.reshape(LANES, channels)

    def swap(x):
        return lax.all_to_all(x.reshape(peers, -1, LANES), plane, 0, 0, tiled=True)

    def pack(arrays, *live):
        parts = len(arrays)
        rows = parts * chp + 16 * len(live)
        (out,) = call(
            functools.partial(pack_body, parts, ch, chp),
            [((peers, rows, LANES), BF)],
            *[flat(x) for x in arrays], *live,
            scratch=[
                pltpu.VMEM((parts, LANES, channels), BF),
                pltpu.VMEM((peers, rows, LANES), BF),
                pltpu.SemaphoreType.DMA((3, parts)),
            ],
            mib=56,
            far_in=range(parts),
            far_out=(0,),
        )
        return out

    sent = pack([key, value, control])
    mine = swap(sent).reshape(peers, 3, chp, LANES)
    wanted = lax.dynamic_index_in_dim(detail_blocks[0], my_col, 0, keepdims=False)
    named = (wanted >= 0) | (jnp.arange(cols) == my_col)
    named = jnp.concatenate([named, jnp.stack([my_z >= 1, my_z + 1 < planes])])
    live = jnp.where(jnp.pad(named, (0, 14 - cols)), 0.0, NEG).astype(F32)
    live = jnp.broadcast_to(live[:, None], (16, LANES))
    sent_q = pack([query, grad_out], live)
    mine, sent_q = lax.optimization_barrier((mine, sent_q))
    rounds = [
        [pair for i in range(start, planes - 1, 2) for pair in ((i, i + 1), (i + 1, i))]
        for start in range(2)
    ]

    def exchange(messages):
        return [lax.ppermute(x, "z", pairs) for x, pairs in zip(messages, rounds)]

    rim = (3 * cols + cols // 2, chp, LANES)
    sides = exchange(call(facing(rim_body, 1), [(rim, BF)] * 2, mine))

    coefs = lax.dynamic_slice_in_dim(kernel.reshape(9, channels), me * ch, ch, 1)
    coefs = jnp.pad(coefs.T, ((0, chp - ch), (0, LANES - 9)))
    queries = swap(sent_q)

    wide = cols * LANES

    def tiles(*lead):
        return lead + (chp, LANES), BF

    mine, part = call(
        own_values_body,
        [(mine.shape, BF), ((cols, chp, LANES), F32)],
        mine, coefs,
        flops=3 * 10**9,
        aliases={0: 0},
    )
    mine, *sides = call(
        facing(values_body, 1, 6),
        [(x.shape, BF) for x in (mine, *sides)],
        mine, *sides, part, coefs,
        flops=4 * 10**9,
        aliases={0: 0, 1: 1, 2: 2},
    )
    side = (2 * cols + cols // 2, chp, LANES)
    flops = 10 * peers * heads * LANES * (wide + 2 * LANES) * 256
    dq, *terms, dk, dv = call(
        facing(functools.partial(attend_body, heads), 2, 5),
        [
            ((peers, chp, LANES), BF),
            (side, BF),
            (side, BF),
            ((ROWS, chp, wide), F32),
            ((ROWS, chp, wide), F32),
        ],
        queries, mine, *sides,
        flops=flops,
        mib=6,
    )
    got_terms = exchange(terms)

    own = ((ROWS, chp, wide), F32)
    sent_dq, dk, dv = call(
        facing(functools.partial(kernel_grad_body, ch), 2, 6),
        [((peers, chp + 32, LANES), BF), own, own],
        dq, mine, *sides, dk, dv, *terms,
        scratch=[
            pltpu.VMEM((9, chp, LANES), F32),
            pltpu.VMEM((peers, 32, LANES), BF),
            pltpu.SemaphoreType.DMA((4,)),
        ],
        far_out=(0, 1, 2),
        hbm=(1, 2),
        flops=4 * 10**9,
    )
    dq_back = swap(sent_dq)

    (results,) = call(
        facing(finish_body, 2, 4), [tiles(peers, 3)],
        *[pltpu.with_memory_space_constraint(x, pltpu.HBM) for x in (dk, dv)],
        *terms, *got_terms, coefs,
        scratch=[
            pltpu.VMEM((ROWS, chp, wide), F32),
            pltpu.VMEM((ROWS, chp, wide), F32),
            pltpu.VMEM(side, BF),
            pltpu.VMEM(side, BF),
            pltpu.VMEM((peers, 3, chp, LANES), BF),
            pltpu.SemaphoreType.DMA((4,)),
            pltpu.SemaphoreType.DMA((chp // 16,)),
        ],
        far_in=(0, 1, 4, 5),
        far_out=(0,),
        flops=4 * 10**9,
    )
    back = swap(results).reshape(peers, 3, chp, LANES)
    sums = (-(-9 * channels // (8 * LANES)) * 8, LANES)
    grad_query, taps_sum = call(
        functools.partial(unpack_query_body, ch, chp),
        [((LANES, channels), BF), (sums, F32)],
        dq_back,
    )
    step = 1
    while 2 * step < planes:
        other = lax.ppermute(taps_sum, "z", [(i, i ^ step) for i in range(planes)])
        (taps_sum,) = call(add_body, [(sums, F32)], taps_sum, other)
        step *= 2
    other = lax.ppermute(taps_sum, "z", [(i, i ^ step) for i in range(planes)])
    (grad_kernel,) = call(taps_out_body, [((3, 3, channels), F32)], taps_sum, other)
    outs = call(functools.partial(unpack_body, ch), [((LANES, channels), BF)] * 3, back)
    return tuple(x.reshape(shape) for x in [grad_query] + list(outs)) + (grad_kernel,)


def solution(mesh):
    trow, tcol = mesh.shape["trow"], mesh.shape["tcol"]
    grid = Mesh(mesh.devices.reshape(trow // ROWS, ROWS, tcol), ("z", "x", "c"))
    tiled = P(("z", "x"), "c", None)
    return jax.shard_map(
        per_device,
        mesh=grid,
        in_specs=(tiled, tiled, tiled, tiled, P(), tiled, P(("z", "x"), None, None)),
        out_specs=(tiled, tiled, tiled, tiled, P()),
        check_vma=False,
    )
```

```python
import functools
import math

import jax
import jax.numpy as jnp
from jax import lax
from jax.experimental import pallas as pl
from jax.experimental.pallas import tpu as pltpu
from jax.sharding import Mesh, PartitionSpec as P

HEADS = 16
HEAD_DIM = 72
ROWS = 2
LANES = 128
HALF = 64
NEG = -1e30
INV_ROOT = HEAD_DIM ** (-0.5)
LOG2E = 1.4426950408889634
BF = jnp.bfloat16
F32 = jnp.float32


def params(mib):
    return pltpu.CompilerParams(vmem_limit_bytes=mib << 20)


ANY = pl.BlockSpec(memory_space=pl.ANY)
VMEM = pl.BlockSpec(memory_space=pltpu.VMEM)


def call(body, outs, *args, scratch=(), flops=0, mib=8, aliases=None, far_in=(), far_out=(), hbm=()):
    moved = sum(a.size * a.dtype.itemsize for a in args)
    moved += sum(math.prod(shape) * jnp.dtype(dtype).itemsize for shape, dtype in outs)
    return pl.pallas_call(
        body,
        out_shape=[
            (pltpu.HBM if n in hbm else jax.ShapeDtypeStruct)(shape, dtype)
            for n, (shape, dtype) in enumerate(outs)
        ],
        in_specs=[ANY if n in far_in else VMEM for n in range(len(args))],
        out_specs=[ANY if n in far_out else VMEM for n in range(len(outs))],
        scratch_shapes=list(scratch),
        input_output_aliases=aliases or {},
        compiler_params=params(mib),
        cost_estimate=pl.CostEstimate(flops=flops, bytes_accessed=moved, transcendentals=0),
    )(*args)


def facing(body, *places):
    def kernel(*refs):
        odd = lax.rem(lax.axis_index("z"), 2)
        turned = list(refs)
        for place in places:
            turned[place], turned[place + 1] = refs[place + 1], refs[place]

        @pl.when(odd == 1)
        def _():
            body(*refs)

        @pl.when(odd == 0)
        def _():
            body(*turned)

    return kernel


def my_halves():
    odd = lax.rem(lax.axis_index("c"), 2)
    return [pl.ds(pl.multiple_of(x * HALF, HALF), HALF) for x in (odd, 1 - odd)]


def store_halves(out, x):
    for i, half in enumerate(my_halves()):
        out[half] = x[i * HALF : (i + 1) * HALF]


def pack_body(parts, ch, chp, *refs):
    ins = refs[:parts]
    live, out = refs[parts:-4], refs[-4]
    held, packed, sems = refs[-3:]
    halves = my_halves()

    def get(n):
        return [
            pltpu.make_async_copy(
                ins[n].at[halves[i]], held.at[n, pl.ds(i * HALF, HALF)], sems.at[i, n]
            )
            for i in range(2)
        ]

    for n in range(parts):
        for copy in get(n):
            copy.start()
    backs = []
    for n in range(parts):
        for copy in get(n):
            copy.wait()
        x = held[n]
        if ch % 16:
            x = x.astype(F32)
        x = x.T
        rows = pl.ds(n * chp, chp)
        for p in range(out.shape[0]):
            piece = x[p * ch : (p + 1) * ch]
            if chp > ch:
                piece = jnp.concatenate([piece, jnp.zeros((chp - ch, LANES), piece.dtype)], axis=0)
            packed[p, n * chp : (n + 1) * chp] = piece.astype(BF)
        if n == parts - 1 and live:
            for p in range(out.shape[0]):
                packed[p, parts * chp :] = live[0][...].astype(BF)
            rows = pl.ds(n * chp, chp + 16)
        backs.append(pltpu.make_async_copy(packed.at[:, rows], out.at[:, rows], sems.at[2, n]))
        backs[n].start()
    for back in backs:
        back.wait()


def unpack_body(ch, x_ref, *outs):
    peers = x_ref.shape[0]
    for n, out in enumerate(outs):
        pieces = [x_ref[p, n] for p in range(peers)]
        if ch % 16:
            pieces = [piece.astype(F32)[:ch] for piece in pieces]
        store_halves(out, jnp.concatenate(pieces, axis=0).T.astype(BF))


def unpack_query_body(ch, chp, x_ref, out, gk_ref):
    peers = x_ref.shape[0]
    pieces = [x_ref[p, :chp] for p in range(peers)]
    if ch % 16:
        pieces = [piece.astype(F32)[:ch] for piece in pieces]
    store_halves(out, jnp.concatenate(pieces, axis=0).T.astype(BF))
    count = out.shape[1] // LANES
    total = [jnp.zeros((16, LANES), F32) for _ in range(count + 2)]
    lane = lax.broadcasted_iota(jnp.int32, (16, LANES), 1)
    for p in range(peers):
        table = x_ref[p, chp:].astype(F32)
        pieces = [table[:16] + pltpu.roll(table, 32 - 9, 0)[:16]]
        if ch > LANES:
            more = pltpu.roll(table, 32 - 18, 0)[:16]
            more = more + pltpu.roll(more, 2 * LANES - ch, 1)
            pieces.append(jnp.where(lane < ch - LANES, more, 0.0))
        first, off = divmod(p * ch, LANES)
        for b, piece in enumerate(pieces):
            turned = pltpu.roll(piece, off, 1) if off else piece
            total[first + b] = total[first + b] + jnp.where(lane >= off, turned, 0.0)
            if off:
                total[first + b + 1] = total[first + b + 1] + jnp.where(lane < off, turned, 0.0)
    gk_ref[...] = jnp.zeros_like(gk_ref)
    for n in range(count):
        gk_ref[9 * n : 9 * n + 9] = total[n][:9]


def taps_out_body(x_ref, y_ref, out):
    total = x_ref[...] + y_ref[...]
    count = out.shape[2] // LANES
    total = jnp.concatenate([total[9 * n : 9 * n + 9] for n in range(count)], axis=1)
    for a in range(3):
        out[a] = total[3 * a : 3 * a + 3]


def add_body(x_ref, y_ref, out):
    out[...] = x_ref[...] + y_ref[...]


def chunks(rows):
    count = rows // 16
    return pl.loop(0, count, unroll=1 if count % 3 else 3)


def second_rows(rows):
    lane = lax.broadcasted_iota(jnp.int32, (rows, LANES), 1)
    return lane >= HALF, lane < HALF


def lane_masks(rows):
    col = lax.broadcasted_iota(jnp.int32, (rows, LANES), 1) & (HALF - 1)
    return second_rows(rows), col == 0, col == HALF - 1


def col_shifts(tiles, masks):
    _, first, last = masks
    none = jnp.zeros_like(tiles[0])
    out = []
    for j, t in enumerate(tiles):
        before = tiles[j - 1] if j else none
        after = tiles[j + 1] if j + 1 < len(tiles) else none
        out.append(
            (
                pltpu.roll(jnp.where(last, before, t), 1, 1),
                t,
                pltpu.roll(jnp.where(first, after, t), LANES - 1, 1),
            )
        )
    return out


def merge(tiles_second, tiles_first, masks):
    second = masks[0]
    return [
        jnp.where(second[j % 2], x, y) for j, (x, y) in enumerate(zip(tiles_second, tiles_first))
    ]


def row_terms(tiles, coef, masks):
    return [
        [sum(coef[3 * a + b] * t[b] for b in range(3)) for a in range(3)]
        for t in col_shifts(tiles, masks)
    ]


def edge_terms(tiles, coef, masks):
    second = masks[0]
    mixed = [[jnp.where(second[p], coef[b], coef[6 + b]) for b in range(3)] for p in range(2)]
    return [
        sum(mixed[j % 2][b] * t[b] for b in range(3))
        for j, t in enumerate(col_shifts(tiles, masks))
    ]


def turn(x):
    return pltpu.roll(x, HALF, 1)


def conv_pair(first, last, edge, coef, masks):
    second = masks[0]
    top, bottom = row_terms(first, coef, masks), row_terms(last, coef, masks)
    out = ([], [])
    for j, ((tu, tm, td), (bu, bm, bd)) in enumerate(zip(top, bottom)):
        e = edge[j] if edge else 0.0
        out[0].append(tm + turn(jnp.where(second[j % 2], e + td, tu + bd)))
        out[1].append(bm + turn(jnp.where(second[j % 2], tu + bd, bu + e)))
    return out


def taps(kc_ref, at):
    block = kc_ref[at, :]
    return [jnp.broadcast_to(block[:, t : t + 1], (16, LANES)) for t in range(9)]


def rim_body(a_ref, up_ref, down_ref):
    cols = a_ref.shape[0] // ROWS
    second = second_rows(a_ref.shape[2])
    for out, row, further, want in ((up_ref, 0, 1, 0), (down_ref, ROWS - 1, ROWS - 2, 1)):
        for j in range(cols):
            for n in range(3):
                out[n * cols + j] = a_ref[row * cols + j, n]
        for m in range(0, cols, 2):
            even, odd = (a_ref[further * cols + m + i, 2].astype(F32) for i in range(2))
            out[3 * cols + m // 2] = jnp.where(second[want], odd, even).astype(BF)


def outer_controls(u_ref, d_ref, at, masks):
    half = u_ref.shape[0] * 2 // 7
    above, below = (
        [ref[3 * half + j // 2, at, :].astype(F32) for j in range(half)] for ref in (u_ref, d_ref)
    )
    return merge(above, below, masks)


def load(ref, first, count, at):
    return [ref[first + j, at, :].astype(F32) for j in range(count)]


def load_own(a_ref, r, n, at):
    cols = a_ref.shape[0] // ROWS
    return [a_ref[r * cols + j, n, at, :].astype(F32) for j in range(cols)]


def own_values_body(a_ref, kc_ref, a_out, part_ref):
    cols = a_ref.shape[0] // ROWS

    @chunks(a_ref.shape[2])
    def _(step):
        at = pl.ds(pl.multiple_of(step * 16, 16), 16)
        masks = lane_masks(16)
        second = masks[0]
        conv = conv_pair(
            load_own(a_ref, 0, 2, at), load_own(a_ref, 1, 2, at), None, taps(kc_ref, at), masks
        )
        for j in range(cols):
            part_ref[j, at, :] = jnp.where(second[j % 2], conv[1][j], conv[0][j])
            for r in range(ROWS):
                tile = r * cols + j
                value = a_ref[tile, 1, at, :].astype(F32)
                inner = second[j % 2] if r == 0 else second[1 - j % 2]
                a_out[tile, 0, at, :] = a_ref[tile, 0, at, :]
                a_out[tile, 1, at, :] = jnp.where(inner, value + conv[r][j], value).astype(BF)
                a_out[tile, 2, at, :] = a_ref[tile, 2, at, :]


def values_body(a_ref, u_ref, d_ref, part_ref, kc_ref, a_out, u_out, d_out):
    cols = a_ref.shape[0] // ROWS

    @chunks(a_ref.shape[2])
    def _(step):
        at = pl.ds(pl.multiple_of(step * 16, 16), 16)
        masks = lane_masks(16)
        second = masks[0]
        coef = taps(kc_ref, at)
        far = edge_terms(outer_controls(u_ref, d_ref, at, masks), coef, masks)
        own = merge(load_own(a_ref, ROWS - 1, 2, at), load_own(a_ref, 0, 2, at), masks)
        own = edge_terms(own, coef, masks)
        above = row_terms(load(u_ref, 2 * cols, cols, at), coef, masks)
        below = row_terms(load(d_ref, 2 * cols, cols, at), coef, masks)
        for ref, out in ((u_ref, u_out), (d_ref, d_out)):
            for n in range(ref.shape[0]):
                if not cols <= n < 2 * cols:
                    out[n, at, :] = ref[n, at, :]
        for j in range(cols):
            (uu, um, ud), (du, dm, dd) = above[j], below[j]
            pick = second[j % 2]
            u_conv = um + turn(jnp.where(pick, far[j] + ud, uu + own[j]))
            d_conv = dm + turn(jnp.where(pick, own[j] + dd, du + far[j]))
            rim = part_ref[j, at, :] + turn(jnp.where(pick, uu, dd))
            u_out[cols + j, at, :] = (u_ref[cols + j, at, :].astype(F32) + u_conv).astype(BF)
            d_out[cols + j, at, :] = (d_ref[cols + j, at, :].astype(F32) + d_conv).astype(BF)
            for r in range(ROWS):
                tile = r * cols + j
                value = a_ref[tile, 1, at, :].astype(F32)
                inner = pick if r == 0 else second[1 - j % 2]
                a_out[tile, 0, at, :] = a_ref[tile, 0, at, :]
                a_out[tile, 1, at, :] = jnp.where(inner, value, value + rim).astype(BF)
                a_out[tile, 2, at, :] = a_ref[tile, 2, at, :]


def attend_body(heads, q_ref, a_ref, u_ref, d_ref, dq_ref, up_ref, down_ref, dk_ref, dv_ref):
    peers = q_ref.shape[0]
    cols = peers // ROWS
    chp = a_ref.shape[2]
    wide = cols * LANES

    dk_ref[...] = jnp.zeros_like(dk_ref)
    dv_ref[...] = jnp.zeros_like(dv_ref)
    chan = lax.broadcasted_iota(jnp.int32, (chp, LANES), 0)
    mine = [(chan >= h * HEAD_DIM) & (chan < (h + 1) * HEAD_DIM) for h in range(heads)]

    def spread(x):
        x = x.astype(F32)
        return jnp.concatenate([jnp.where(m, x, 0.0) for m in mine], axis=1).astype(BF)

    def dot(x, y, on_x, on_y):
        return lax.dot_general(
            x, y, (((on_x,), (on_y,)), ((), ())), preferred_element_type=F32
        )

    def front(tile):
        r, j = divmod(tile, cols)
        q = spread(q_ref[tile, :chp])
        g = spread(q_ref[tile, chp : 2 * chp])

        def all_keys(n):
            above = u_ref[n * cols + j] if r == 0 else a_ref[tile - cols, n]
            below = d_ref[n * cols + j] if r == ROWS - 1 else a_ref[tile + cols, n]
            row = [a_ref[r * cols + p, n] for p in range(cols)]
            return jnp.concatenate(row + [above, below], axis=1)

        k = all_keys(0)
        return q, g, k, dot(q, k, 0, 0), dot(g, all_keys(1), 0, 0)

    def middle(tile, s, gw):
        r = tile // cols
        live = q_ref[tile, 2 * chp :].astype(F32)
        zero = jnp.zeros((1, LANES), F32)
        bias = jnp.concatenate(
            [live[p : p + 1] for p in range(cols)]
            + [
                live[cols : cols + 1] if r == 0 else zero,
                live[cols + 1 : cols + 2] if r == ROWS - 1 else zero,
            ],
            axis=1,
        )
        s = s + bias
        top = jnp.max(s, axis=1, keepdims=True)
        e = jnp.exp2((s - top) * (INV_ROOT * LOG2E))
        w = e * (1.0 / jnp.sum(e, axis=1, keepdims=True))
        delta = jnp.sum(w * gw, axis=1, keepdims=True)
        return w.astype(BF), (w * (gw - delta)).astype(BF)

    def back(tile, q, g, k, w, gs):
        r, j = divmod(tile, cols)
        span = slice(j * LANES, (j + 1) * LANES)
        dk = dot(q, gs, 1, 0)
        dv = dot(g, w, 1, 0)
        dq = dot(k, gs, 1, 1)
        own = dq[:, :LANES]
        for h in range(1, heads):
            own = jnp.where(mine[h], dq[:, h * LANES : (h + 1) * LANES], own)
        dq_ref[tile] = (own * INV_ROOT).astype(BF)
        dk_ref[r] += dk[:, :wide]
        dv_ref[r] += dv[:, :wide]
        for side, at in ((r - 1, wide), (r + 1, wide + LANES)):
            dk_side, dv_side = dk[:, at : at + LANES], dv[:, at : at + LANES]
            if 0 <= side < ROWS:
                dk_ref[side, :, span] += dk_side
                dv_ref[side, :, span] += dv_side
            else:
                out = up_ref if side < 0 else down_ref
                out[j] = (dk_side * INV_ROOT).astype(BF)
                out[cols + j] = dv_side.astype(BF)

    ahead = front(0)
    for tile in range(peers):
        q, g, k, s, gw = ahead
        if tile + 1 < peers:
            ahead = front(tile + 1)
        halves = [middle(tile, s[i : i + 64], gw[i : i + 64]) for i in range(0, s.shape[0], 64)]
        w, gs = (jnp.concatenate(x, axis=0) for x in zip(*halves))
        back(tile, q, g, k, w, gs)

    second = second_rows(chp)
    for out, row, want in ((up_ref, 0, 0), (down_ref, ROWS - 1, 1)):
        for m in range(0, cols, 2):
            even, odd = (dv_ref[row, :, (m + i) * LANES : (m + i + 1) * LANES] for i in range(2))
            out[2 * cols + m // 2] = jnp.where(second[1 - want], even, odd).astype(BF)


def value_terms(dv_ref, up_ref, down_ref, i, j, at):
    cols = dv_ref.shape[2] // LANES
    if i == 0:
        return up_ref[cols + j, at, :].astype(F32)
    if i == ROWS + 1:
        return down_ref[cols + j, at, :].astype(F32)
    return dv_ref[i - 1, at, j * LANES : (j + 1) * LANES]


def kernel_grad_body(
    ch, dq_ref, a_ref, u_ref, d_ref, dk_ref, dv_ref, up_ref, down_ref, out_ref, dk_out, dv_out, sums, rows, sems
):
    cols = dv_ref.shape[2] // LANES
    chp = dv_ref.shape[1]
    copies = [
        pltpu.make_async_copy(dq_ref, out_ref.at[:, pl.ds(0, chp)], sems.at[0]),
        pltpu.make_async_copy(dk_ref, dk_out, sems.at[1]),
        pltpu.make_async_copy(dv_ref, dv_out, sems.at[2]),
    ]
    for copy in copies:
        copy.start()

    @chunks(chp)
    def _(step):
        at = pl.ds(pl.multiple_of(step * 16, 16), 16)
        masks = lane_masks(16)
        second = masks[0]
        acc = [jnp.zeros((16, LANES), F32) for _ in range(9)]
        outer = col_shifts(outer_controls(u_ref, d_ref, at, masks), masks)
        above, here = outer, col_shifts(load(u_ref, 2 * cols, cols, at), masks)
        for i in range(ROWS + 2):
            if i < ROWS:
                below = col_shifts(load_own(a_ref, i, 2, at), masks)
            elif i == ROWS:
                below = col_shifts(load(d_ref, 2 * cols, cols, at), masks)
            else:
                below = outer
            for j in range(cols):
                g = value_terms(dv_ref, up_ref, down_ref, i, j, at)
                turned = turn(g)
                for b in range(3):
                    acc[b] += jnp.where(second[j % 2], above[j][b], here[j][b]) * turned
                    acc[3 + b] += here[j][b] * g
                    acc[6 + b] += jnp.where(second[j % 2], here[j][b], below[j][b]) * turned
            above, here = here, below
        for n in range(9):
            sums[n, at, :] = acc[n]

    lane = lax.broadcasted_iota(jnp.int32, (chp, LANES), 1)
    whole = jnp.zeros((chp, LANES), F32)
    for t in range(9):
        whole = jnp.where(lane == t, jnp.sum(sums[t], axis=1, keepdims=True), whole)
    def split(x):
        high = x.astype(BF).astype(F32)
        return high, x - high

    high, low = split(whole[: min(chp, LANES)])
    table = high + pltpu.roll(low, 9, 1)
    if chp < LANES:
        table = jnp.concatenate([table, jnp.zeros((LANES - chp, LANES), F32)], axis=0)
    if chp > LANES:
        more = jnp.concatenate(split(whole[LANES:]), axis=0)
        more = jnp.concatenate([more, jnp.zeros((LANES - more.shape[0], LANES), F32)], axis=0)
        table = table + pltpu.roll(more, 18, 1)
    table = table.T[:32].astype(BF)
    for tile in range(rows.shape[0]):
        rows[tile] = table
    sums_out = pltpu.make_async_copy(rows, out_ref.at[:, pl.ds(chp, 32)], sems.at[3])
    sums_out.start()
    for copy in copies + [sums_out]:
        copy.wait()


def finish_body(
    dk_hbm, dv_hbm, up_ref, down_ref, u_hbm, d_hbm, kc_ref, out_ref, dk_ref, dv_ref, u_ref, d_ref, held, sems, ends
):
    cols = held.shape[0] // ROWS
    chp = held.shape[2]

    def chunk(step):
        return pl.ds(pl.multiple_of(step * 16, 16), 16)

    def put(step):
        at = chunk(step)
        return pltpu.make_async_copy(held.at[:, :, at], out_ref.at[:, :, at], ends.at[step])

    def get(step):
        at = chunk(step)
        return [
            pltpu.make_async_copy(far.at[:, at], near.at[:, at], sems.at[n, step])
            for n, (far, near) in enumerate(
                ((u_hbm, u_ref), (d_hbm, d_ref), (dv_hbm, dv_ref), (dk_hbm, dk_ref))
            )
        ]

    @pl.loop(0, chp // 16)
    def _(step):
        for copy in get(step):
            copy.start()

    @pl.loop(0, chp // 16)
    def _(step):
        for copy in get(step):
            copy.wait()
        at = chunk(step)
        masks = lane_masks(16)
        coef = taps(kc_ref, at)[::-1]

        def from_side(ref, n):
            return ref[n, at, :].astype(F32)

        def rounded(x):
            return x.astype(BF).astype(F32)

        rows = []
        for i in range(ROWS + 2):
            row = []
            for j in range(cols):
                x = value_terms(dv_ref, up_ref, down_ref, i, j, at)
                if i == 0:
                    rim = from_side(u_ref, 2 * cols + j // 2)
                    x = x + rim
                elif i == ROWS + 1:
                    rim = from_side(d_ref, 2 * cols + j // 2)
                    x = x + rim
                else:
                    if i == 1:
                        x = x + from_side(u_ref, cols + j)
                    if i == ROWS:
                        x = x + from_side(d_ref, cols + j)
                row.append(rounded(x))
            rows.append(row)
        edge = edge_terms(merge(rows[0], rows[-1], masks), coef, masks)
        conv = conv_pair(rows[1], rows[2], edge, coef, masks)
        for r in range(ROWS):
            for j in range(cols):
                tile = r * cols + j
                k = dk_ref[r, at, j * LANES : (j + 1) * LANES] * INV_ROOT
                if r == 0:
                    k = k + from_side(u_ref, j)
                if r == ROWS - 1:
                    k = k + from_side(d_ref, j)
                held[tile, 0, at, :] = k.astype(BF)
                held[tile, 1, at, :] = rows[r + 1][j].astype(BF)
                held[tile, 2, at, :] = conv[r][j].astype(BF)
        put(step).start()

    @pl.loop(0, chp // 16)
    def _(step):
        put(step).wait()


def per_device(query, key, value, control, kernel, grad_out, detail_blocks):
    shape = query.shape
    channels = shape[2]
    planes = lax.axis_size("z")
    cols = lax.axis_size("c")
    peers = ROWS * cols
    heads = HEADS // peers
    ch = heads * HEAD_DIM
    chp = -(-ch // 16) * 16
    plane = ("x", "c")
    my_z = lax.axis_index("z")
    my_col = lax.axis_index("c")
    me = lax.axis_index("x") * cols + my_col

    def flat(x):
        return x.reshape(LANES, channels)

    def swap(x):
        return lax.all_to_all(x.reshape(peers, -1, LANES), plane, 0, 0, tiled=True)

    def pack(arrays, *live):
        parts = len(arrays)
        rows = parts * chp + 16 * len(live)
        (out,) = call(
            functools.partial(pack_body, parts, ch, chp),
            [((peers, rows, LANES), BF)],
            *[flat(x) for x in arrays], *live,
            scratch=[
                pltpu.VMEM((parts, LANES, channels), BF),
                pltpu.VMEM((peers, rows, LANES), BF),
                pltpu.SemaphoreType.DMA((3, parts)),
            ],
            mib=56,
            far_in=range(parts),
            far_out=(0,),
        )
        return out

    sent = pack([key, value, control])
    mine = swap(sent).reshape(peers, 3, chp, LANES)
    wanted = lax.dynamic_index_in_dim(detail_blocks[0], my_col, 0, keepdims=False)
    named = (wanted >= 0) | (jnp.arange(cols) == my_col)
    named = jnp.concatenate([named, jnp.stack([my_z >= 1, my_z + 1 < planes])])
    live = jnp.where(jnp.pad(named, (0, 14 - cols)), 0.0, NEG).astype(F32)
    live = jnp.broadcast_to(live[:, None], (16, LANES))
    sent_q = pack([query, grad_out], live)
    mine, sent_q = lax.optimization_barrier((mine, sent_q))
    rounds = [
        [pair for i in range(start, planes - 1, 2) for pair in ((i, i + 1), (i + 1, i))]
        for start in range(2)
    ]

    def exchange(messages):
        return [lax.ppermute(x, "z", pairs) for x, pairs in zip(messages, rounds)]

    rim = (3 * cols + cols // 2, chp, LANES)
    sides = exchange(call(facing(rim_body, 1), [(rim, BF)] * 2, mine))

    coefs = lax.dynamic_slice_in_dim(kernel.reshape(9, channels), me * ch, ch, 1)
    coefs = jnp.pad(coefs.T, ((0, chp - ch), (0, LANES - 9)))
    queries = swap(sent_q)

    wide = cols * LANES

    def tiles(*lead):
        return lead + (chp, LANES), BF

    mine, part = call(
        own_values_body,
        [(mine.shape, BF), ((cols, chp, LANES), F32)],
        mine, coefs,
        flops=3 * 10**9,
        aliases={0: 0},
    )
    mine, *sides = call(
        facing(values_body, 1, 6),
        [(x.shape, BF) for x in (mine, *sides)],
        mine, *sides, part, coefs,
        flops=4 * 10**9,
        aliases={0: 0, 1: 1, 2: 2},
    )
    side = (2 * cols + cols // 2, chp, LANES)
    flops = 10 * peers * heads * LANES * (wide + 2 * LANES) * 256
    dq, *terms, dk, dv = call(
        facing(functools.partial(attend_body, heads), 2, 5),
        [
            ((peers, chp, LANES), BF),
            (side, BF),
            (side, BF),
            ((ROWS, chp, wide), F32),
            ((ROWS, chp, wide), F32),
        ],
        queries, mine, *sides,
        flops=flops,
        mib=6,
    )
    got_terms = exchange(terms)

    own = ((ROWS, chp, wide), F32)
    sent_dq, dk, dv = call(
        facing(functools.partial(kernel_grad_body, ch), 2, 6),
        [((peers, chp + 32, LANES), BF), own, own],
        dq, mine, *sides, dk, dv, *terms,
        scratch=[
            pltpu.VMEM((9, chp, LANES), F32),
            pltpu.VMEM((peers, 32, LANES), BF),
            pltpu.SemaphoreType.DMA((4,)),
        ],
        far_out=(0, 1, 2),
        hbm=(1, 2),
        flops=4 * 10**9,
    )
    dq_back = swap(sent_dq)

    (results,) = call(
        facing(finish_body, 2, 4), [tiles(peers, 3)],
        *[pltpu.with_memory_space_constraint(x, pltpu.HBM) for x in (dk, dv)],
        *terms, *got_terms, coefs,
        scratch=[
            pltpu.VMEM((ROWS, chp, wide), F32),
            pltpu.VMEM((ROWS, chp, wide), F32),
            pltpu.VMEM(side, BF),
            pltpu.VMEM(side, BF),
            pltpu.VMEM((peers, 3, chp, LANES), BF),
            pltpu.SemaphoreType.DMA((4, chp // 16)),
            pltpu.SemaphoreType.DMA((chp // 16,)),
        ],
        far_in=(0, 1, 4, 5),
        far_out=(0,),
        flops=4 * 10**9,
    )
    back = swap(results).reshape(peers, 3, chp, LANES)
    sums = (-(-9 * channels // (8 * LANES)) * 8, LANES)
    grad_query, taps_sum = call(
        functools.partial(unpack_query_body, ch, chp),
        [((LANES, channels), BF), (sums, F32)],
        dq_back,
    )
    step = 1
    while 2 * step < planes:
        other = lax.ppermute(taps_sum, "z", [(i, i ^ step) for i in range(planes)])
        (taps_sum,) = call(add_body, [(sums, F32)], taps_sum, other)
        step *= 2
    other = lax.ppermute(taps_sum, "z", [(i, i ^ step) for i in range(planes)])
    (grad_kernel,) = call(taps_out_body, [((3, 3, channels), F32)], taps_sum, other)
    outs = call(functools.partial(unpack_body, ch), [((LANES, channels), BF)] * 3, back)
    return tuple(x.reshape(shape) for x in [grad_query] + list(outs)) + (grad_kernel,)


def solution(mesh):
    trow, tcol = mesh.shape["trow"], mesh.shape["tcol"]
    grid = Mesh(mesh.devices.reshape(trow // ROWS, ROWS, tcol), ("z", "x", "c"))
    tiled = P(("z", "x"), "c", None)
    return jax.shard_map(
        per_device,
        mesh=grid,
        in_specs=(tiled, tiled, tiled, tiled, P(), tiled, P(("z", "x"), None, None)),
        out_specs=(tiled, tiled, tiled, tiled, P()),
        check_vma=False,
    )
```
